256 devices in a mesh: ctx: 128 (over z, x, y), head: 2 (over core).
Axes of the slice: x: 4, y: 4, z: 8, core: 2. Of those that a mesh axis runs over, the one named last changes fastest.
Arguments:
- q_home: bfloat16 [65536, 2048], P('ctx', 'head'), may hold values from -18 to 18
- k_home: bfloat16 [65536, 512], P('ctx', 'head'), may hold values from -6 to 6
- value_slots_local: bfloat16 [65536, 512], P('ctx', 'head'), may hold values from -16 to 16
- out_weight: bfloat16 [2048, 4096], P('head'), may hold values from -0.125 to 0.125
- router: float32 [65536], P('ctx'), may hold values from 0.25 to 1
- positions: int32 [65536], P('ctx'), may hold values from 0 to 262143, as said below
- counts: int32 [128], P('ctx'), may hold values from 1 to 512, 16384 in all
Outputs:
- routed_update: bfloat16 [65536, 4096], P('ctx', 'head')
The draws below stay inside these ranges and needn't reach their ends.
Inputs may be any that keep to these rules, and one draw needn't show every extreme that they name: counts sum to 16384; the busiest shard holds exactly 512. The 512 positions of shard d are distinct, increasing, and lie in [d * 2048, (d + 1) * 2048).
All inputs are finite; a program needn't handle non-finite values.
Results may differ from the reference program's by a relative error of at most 0.033.
Values may be sent and summed in bfloat16 or wider, within the bound.
No kernel may reach another device: no remote copies, remote signals or barrier semaphores. Data moves between devices by JAX's collectives and lax.ppermute only.
A program may use at most 128 MiB of HBM per device.

```python
import math
import jax
import jax.numpy as jnp
import numpy as np
from jax import lax

D = 4096
QUERY_HEADS = 16
KEY_VALUE_HEADS = 4
HEAD_WIDTH = 128
PICKED_PER_SHARD = 128
TOK_DEV = 2048
SLOT_CAPACITY = 512
SHARD_COUNT = 128
PICKED_OVERALL = 16384


def slot_positions(key):
    base_key = jax.random.fold_in(key, 11)
    shard_keys = jax.random.split(base_key, SHARD_COUNT)
    chosen = jax.vmap(lambda one_key: jax.random.permutation(one_key, TOK_DEV)[:SLOT_CAPACITY])(shard_keys)
    ordered = jnp.sort(chosen, axis=1) + (jnp.arange(SHARD_COUNT) * TOK_DEV)[:, None]
    return ordered.reshape(-1).astype(jnp.int32)


def draw_positions(key, part):
    return slot_positions(key)


def draw_q_home(key, part):
    count_of_rows = SHARD_COUNT * SLOT_CAPACITY
    value_rows = jnp.clip(2.5 * jax.random.normal(jax.random.fold_in(key, 23), (count_of_rows, QUERY_HEADS * HEAD_WIDTH), jnp.float32), -15.0, 15.0)
    return value_rows.astype(jnp.bfloat16)


def draw_k_home(key, part):
    count_of_rows = SHARD_COUNT * SLOT_CAPACITY
    value_rows = jnp.clip(jax.random.normal(jax.random.fold_in(key, 33), (count_of_rows, KEY_VALUE_HEADS * HEAD_WIDTH), jnp.float32), -6.0, 6.0)
    return value_rows.astype(jnp.bfloat16)


def block_scale(own_key, shape, cuts, least, top_value):
    gain, own = 1.0, jax.random.fold_in(own_key, 6)
    for position, shards_of in cuts:
        draws = jnp.exp(jax.random.uniform(jax.random.fold_in(own, position), (shards_of,), jnp.float32, least / len(cuts), top_value / len(cuts)))
        gain = gain * jnp.repeat(draws, shape[position] // shards_of).reshape([-1 if axis == position else 1 for axis in range(len(shape))])
    return gain


def split_up(count, total, reach, slope):
    portions = [(1 << 20) // math.isqrt(standing ** slope) + 1 for standing in range(2, count + 1)]
    rest, given = total - reach - (count - 1), [1] * (count - 1)
    while rest > 0:
        movable = [i for i in range(count - 1) if given[i] < reach]
        pool, left = sum([portions[i] for i in movable]), rest
        for i in movable:
            more = min(reach - given[i], max(1, left * portions[i] // pool), rest)
            given[i] = given[i] + more
            rest = rest - more
    return np.array([reach] + given)


def uneven(stream_key, count, total, bound, slope):
    if count == 2:
        one = jax.random.randint(stream_key, (), max(1, total - bound), min(bound, total - 1) + 1)
        return jnp.stack([one, total - one])
    tallies = jnp.asarray(split_up(count, total, bound, slope), jnp.int32)
    pairs = (count - 1) // 2
    donor, taker = tallies[1:1 + 2 * pairs:2], tallies[2:2 + 2 * pairs:2]
    room = jnp.minimum(donor - 1, bound - taker)
    moved = jax.random.randint(jax.random.fold_in(stream_key, 1), (pairs,), 0, 1 << 20) % (room + 1)
    tallies = tallies.at[1:1 + 2 * pairs:2].set(donor - moved).at[2:2 + 2 * pairs:2].set(taker + moved)
    return tallies[jax.random.permutation(jax.random.fold_in(stream_key, 2), count)]


def normal_values(own_key, dims, spread, most, shards=(), kind=jnp.bfloat16):
    factor_of = block_scale(own_key, dims, shards, -0.22, 0.18) if shards else 1.0
    array = jax.random.normal(own_key, dims, jnp.float32) * spread * factor_of
    return jnp.minimum(jnp.maximum(array, -most), most).astype(kind)


def setup_inputs(seed: int = 0) -> dict:
    keys = jax.random.split(jax.random.key(seed), 8)
    return {
        "q_home": draw_q_home(jax.random.fold_in(keys[7], 71), 0),
        "k_home": draw_k_home(jax.random.fold_in(keys[7], 71), 0),
        "value_slots_local": normal_values(keys[2], (SHARD_COUNT * SLOT_CAPACITY, KEY_VALUE_HEADS * HEAD_WIDTH), 3.0, 16.0, ((0, 128), (1, 2))),
        "out_weight": normal_values(keys[3], (QUERY_HEADS * HEAD_WIDTH, D), (QUERY_HEADS * HEAD_WIDTH) ** -0.5, 0.125, ((0, 2),)),
        "router": jnp.clip(jnp.exp(math.log(1.0) - 1.3862944 * jax.random.uniform(keys[4], (SHARD_COUNT * SLOT_CAPACITY,), jnp.float32) ** block_scale(keys[4], (SHARD_COUNT * SLOT_CAPACITY,), ((0, 128),), -0.2, 0.2)), 0.25, 1.0),
        "positions": draw_positions(jax.random.fold_in(keys[7], 71), 0),
        "counts": uneven(keys[6], SHARD_COUNT, PICKED_OVERALL, SLOT_CAPACITY, 2).astype(jnp.int32),
    }


rope_theta = 500000.0


def inverse_freqs():
    half_dim = HEAD_WIDTH // 2
    return rope_theta ** (-(jnp.arange(half_dim, dtype=jnp.float32) * 2.0 / HEAD_WIDTH))


def rotate_heads(value_rows, positions):
    heads = value_rows.shape[1] // HEAD_WIDTH
    half_dim = HEAD_WIDTH // 2
    inputs = value_rows.astype(jnp.float32).reshape(value_rows.shape[0], heads, HEAD_WIDTH)
    angles = positions.astype(jnp.float32)[:, None] * inverse_freqs()[None, :]
    cosine = jnp.cos(angles)[:, None, :]
    sine = jnp.sin(angles)[:, None, :]
    first = inputs[..., :half_dim]
    second = inputs[..., half_dim:]
    rotated = jnp.concatenate([first * cosine - second * sine, second * cosine + first * sine], axis=-1)
    return rotated.reshape(value_rows.shape).astype(jnp.bfloat16)


def reference(q_home, k_home, value_slots_local, out_weight, router, positions, counts):
    shard_total = counts.shape[0]
    offsets = (jnp.cumsum(counts) - counts).astype(jnp.int32)
    selected = jnp.arange(PICKED_OVERALL, dtype=jnp.int32)
    below = offsets[None, :] <= selected[:, None]
    source = (jnp.sum(below.astype(jnp.int32), axis=1) - 1).astype(jnp.int32)
    start_of = jnp.max(jnp.where(below, offsets[None, :], 0), axis=1).astype(jnp.int32)
    home_rows = (source * SLOT_CAPACITY + selected - start_of).astype(jnp.int32)
    sel_positions = jnp.take(positions, home_rows, axis=0)
    q_sel = rotate_heads(jnp.take(q_home, home_rows, axis=0), sel_positions)
    picked_keys = rotate_heads(jnp.take(k_home, home_rows, axis=0), sel_positions)
    picked_values = jnp.take(value_slots_local, home_rows, axis=0)
    group_width = QUERY_HEADS // KEY_VALUE_HEADS
    gathered_keys = picked_keys.astype(jnp.float32).reshape(PICKED_OVERALL, KEY_VALUE_HEADS, HEAD_WIDTH)
    gathered_values = picked_values.astype(jnp.float32).reshape(PICKED_OVERALL, KEY_VALUE_HEADS, HEAD_WIDTH)
    scale = 1.0 / (HEAD_WIDTH ** 0.5)

    def block_attend(block_index):
        first_row = block_index * PICKED_PER_SHARD
        query_block = lax.dynamic_slice_in_dim(q_sel, first_row, PICKED_PER_SHARD, 0)
        query_block = query_block.astype(jnp.float32).reshape(PICKED_PER_SHARD, KEY_VALUE_HEADS, group_width, HEAD_WIDTH)
        query_ids = first_row + jnp.arange(PICKED_PER_SHARD, dtype=jnp.int32)
        scores = jnp.einsum("bkgd,nkd->bkgn", query_block, gathered_keys) * scale
        visible = selected[None, None, None, :] <= query_ids[:, None, None, None]
        maxima = jnp.max(jnp.where(visible, scores, -1e30), axis=-1)
        exp_terms = jnp.where(visible, jnp.exp(scores - maxima[..., None]), 0.0)
        totals = jnp.sum(exp_terms, axis=-1)
        probs = lax.optimization_barrier(exp_terms.astype(jnp.bfloat16)).astype(jnp.float32)
        weighted = jnp.einsum("bkgn,nkd->bkgd", probs, gathered_values)
        attended_block = weighted / totals[..., None]
        return attended_block.reshape(PICKED_PER_SHARD, QUERY_HEADS * HEAD_WIDTH).astype(jnp.bfloat16)

    attended = lax.map(block_attend, jnp.arange(shard_total, dtype=jnp.int32))
    attended = attended.reshape(PICKED_OVERALL, QUERY_HEADS * HEAD_WIDTH)
    summed = jnp.dot(attended, out_weight, preferred_element_type=jnp.float32).astype(jnp.bfloat16)
    scaled = (jnp.take(router, home_rows, axis=0)[:, None] * summed.astype(jnp.float32)).astype(jnp.bfloat16)
    update = jnp.zeros((shard_total * SLOT_CAPACITY, D), jnp.bfloat16).at[home_rows].set(scaled)
    return update
```

```python
import functools

import jax
import jax.numpy as jnp
import numpy as np
from jax import lax
from jax.experimental import pallas as pl
from jax.experimental.pallas import tpu as pltpu
from jax.sharding import PartitionSpec as P

HEAD_WIDTH = 128
THETA = 500000.0
GROUPS = 64
CAP = 320
SLOTS = 8
SHARDS = 128
ROWS = 512
QT = 64
KT = 32
NQ = CAP // QT
NK = CAP // KT
BIG = 1 << 30
BF = jnp.bfloat16
F32 = jnp.float32
SCALE2 = float(1.0 / np.sqrt(128.0) * np.log2(np.e))
VMEM = pl.BlockSpec(memory_space=pltpu.VMEM)
SMEM = pl.BlockSpec(memory_space=pltpu.SMEM)


def params(mib):
    return pltpu.CompilerParams(vmem_limit_bytes=mib * 2**20)


def perm_of(axis, k):
    pairs = []
    for d in range(SHARDS):
        z, x, y = d // 16, d // 4 % 4, d % 4
        if axis == "z":
            z = (z + k) % 8
        elif axis == "x":
            x = (x + k) % 4
        else:
            y = y ^ 1
        pairs.append((d, z * 16 + x * 4 + y))
    return pairs


def hop(a, axis, k=1):
    return lax.ppermute(a, "ctx", perm_of(axis, k))


def ring(a, axis, size, row_dim):
    half = a.shape[row_dim] // 2
    out, up, down = [a], a, a
    for _ in range(size // 2 - 1):
        up, down = hop(up, axis, 1), hop(down, axis, -1)
        out += [up, down]
    lo = hop(lax.slice_in_dim(up, 0, half, axis=row_dim), axis, 1)
    hi = hop(lax.slice_in_dim(down, half, 2 * half, axis=row_dim), axis, -1)
    out.append(jnp.concatenate([lo, hi], axis=row_dim))
    return jnp.stack(out)


def ring_steps(size):
    steps = [0]
    for i in range(1, size // 2):
        steps += [-i, i]
    return steps + [size // 2]


def pack_matrix(rot, transpose):
    packed_dim = 1 if transpose else 0
    o = lax.broadcasted_iota(jnp.int32, (ROWS, ROWS), packed_dim)
    s = lax.broadcasted_iota(jnp.int32, (ROWS, ROWS), 1 - packed_dim)
    src = (o & 7) * 64 + (((o >> 3) + 64 - rot) & 63)
    return jnp.where(src == s, 1.0, 0.0).astype(BF)


def pack_kernel(rot_ref, q_ref, k_ref, v_ref, cos_ref, sin_ref, kv_ref, qp_ref):
    cos, sin = cos_ref[...], sin_ref[...]

    def rotate(x):
        x = x.astype(F32)
        return (x * cos + pltpu.roll(x, 64, 1) * sin).astype(BF)

    m = pack_matrix(rot_ref[0], False)
    for h in range(2):
        k = rotate(k_ref[:, h * 128 : (h + 1) * 128])
        v = v_ref[:, h * 128 : (h + 1) * 128]
        for c, x in ((0, k), (1, v)):
            y = jnp.dot(m, x, preferred_element_type=F32).astype(BF)
            kv_ref[:, h, :, c * 128 : (c + 1) * 128] = y.reshape(32, 16, 128)
        for g in range(4):
            x = rotate(q_ref[:, h * 512 + g * 128 : h * 512 + (g + 1) * 128])
            y = jnp.dot(m, x, preferred_element_type=F32).astype(BF)
            qp_ref[:, h, :, g * 128 : (g + 1) * 128] = y.reshape(32, 16, 128)


def compact_matrix(pos):
    p = lax.broadcasted_iota(jnp.int32, (CAP, SHARDS * SLOTS), 0)
    return jnp.where(p == pos, 1.0, 0.0).astype(BF)


def compact_kernel(pos_ref, kv_ref, k_ref, v_ref):
    y = jnp.dot(compact_matrix(pos_ref[...]), kv_ref[...], preferred_element_type=F32).astype(BF)
    k_ref[...] = y[:, :128]
    v_ref[...] = y[:, 128:]


def attend_kernel(
    nvis_ref, nfull_ref, pos_ref, post_ref, qid_ref, kid_ref, q_ref, k_ref, v_ref, out_ref,
    qs_ref, ob_ref, m_ref, acc_ref,
):
    y = jnp.dot(compact_matrix(pos_ref[...]), q_ref[...], preferred_element_type=F32).astype(BF)
    for i in range(NQ):
        for g in range(4):
            qs_ref[i, g * QT : (g + 1) * QT, :] = y[i * QT : (i + 1) * QT, g * 128 : (g + 1) * 128]
    ones = jnp.ones((8 * KT, 128), BF)

    def tile(i, _):
        m_ref[...] = jnp.full_like(m_ref, -1e30)
        acc_ref[...] = jnp.zeros_like(acc_ref)

        def step(masked, n, _):
            j, dz = n >> 2, n & 3
            r = pl.multiple_of(j * KT, KT)
            key = k_ref[pl.ds(dz * 2, 2), :, pl.ds(r, KT), :].reshape(16 * KT, 128)
            s = lax.dot_general(qs_ref[i], key, (((1,), (1,)), ((), ())), preferred_element_type=F32)
            if masked:
                s = jnp.where(kid_ref[dz, j] <= qid_ref[i], s, -1e30)
            old = m_ref[...]
            new = jnp.maximum(old, jnp.max(s, axis=1, keepdims=True))
            p = jnp.exp2((s - new) * SCALE2).astype(BF)
            keep = jnp.exp2((old - new) * SCALE2)
            add = None
            for c in range(2):
                val = v_ref[:, dz * 2 + c, pl.ds(r, KT), :].reshape(8 * KT, 128)
                val = jnp.concatenate([val, ones], axis=1)
                part = jnp.dot(p[:, c * 8 * KT : (c + 1) * 8 * KT], val, preferred_element_type=F32)
                add = part if add is None else add + part
            acc_ref[...] = acc_ref[...] * keep + add
            m_ref[...] = new
            return 0

        full, vis = nfull_ref[i] * 4, nvis_ref[i] * 4
        lax.fori_loop(0, full, functools.partial(step, False), 0)
        lax.fori_loop(full, vis, functools.partial(step, True), 0)
        acc = acc_ref[...]
        total = acc[:, 128:]
        o = (acc[:, :128] / jnp.where(total > 0.0, total, 1.0)).astype(BF)
        row = pl.multiple_of(i * QT, QT)
        for g in range(4):
            ob_ref[pl.ds(row, QT), g * 128 : (g + 1) * 128] = o[g * QT : (g + 1) * QT]
        return 0

    lax.fori_loop(0, NQ, tile, 0)
    p = lax.broadcasted_iota(jnp.int32, (SHARDS * SLOTS, CAP), 1)
    spread = jnp.where(p == post_ref[...], 1.0, 0.0).astype(BF)
    out_ref[...] = jnp.dot(spread, ob_ref[...], preferred_element_type=F32).astype(BF)


def home_kernel(rot_ref, o_ref, out_ref):
    m = pack_matrix(rot_ref[0], True)
    for h in range(2):
        x = o_ref[:, h, :, :].reshape(ROWS, 512)
        out_ref[:, h * 512 : (h + 1) * 512] = jnp.dot(m, x, preferred_element_type=F32).astype(BF)


def project_kernel(hd_ref, own_ref, other_ref, wa_ref, wb_ref, gain_ref, live_ref, out_ref):
    s = jnp.dot(own_ref[...], wa_ref[...], preferred_element_type=F32)
    s = s + jnp.dot(other_ref[...], wb_ref[...], preferred_element_type=F32)
    s = s.astype(BF).astype(F32)
    out_ref[...] = jnp.where(live_ref[...] > 0, gain_ref[...] * s, 0.0).astype(BF)


def local(q_home, k_home, v_home, weight, router, positions, counts):
    d = lax.axis_index("ctx").astype(jnp.int32)
    hd = lax.axis_index("head").astype(jnp.int32)
    half_w = weight.shape[1] // 2

    theirs = lax.dynamic_slice_in_dim(weight, (1 - hd) * half_w, half_w, axis=1)
    w_other = lax.ppermute(theirs, "head", [(0, 1), (1, 0)])

    freqs = THETA ** (-(jnp.arange(64, dtype=F32) * 2.0 / HEAD_WIDTH))
    angles = positions.astype(F32)[:, None] * jnp.concatenate([freqs, freqs])[None, :]
    sign = jnp.where(jnp.arange(128) < 64, -1.0, 1.0).astype(F32)
    cos, sin = jnp.cos(angles), jnp.sin(angles) * sign[None, :]
    rot = (d % 64).reshape(1)

    kv_packed, q_packed = pl.pallas_call(
        pack_kernel,
        out_shape=(
            jax.ShapeDtypeStruct((32, 2, 16, 256), BF),
            jax.ShapeDtypeStruct((32, 2, 16, 512), BF),
        ),
        in_specs=[SMEM] + [VMEM] * 5,
        out_specs=(VMEM, VMEM),
        compiler_params=params(32),
        name="pack",
    )(rot, q_home, k_home, v_home, cos, sin)
    kv_got = lax.all_to_all(kv_packed.reshape(1024, 256), "ctx", 0, 0, tiled=True)
    q_got = lax.all_to_all(q_packed.reshape(1024, 512), "ctx", 0, 0, tiled=True)
    all_counts = lax.all_gather(counts, "ctx", axis=0, tiled=True)

    z, x, yl = d // 16, d // 4 % 4, d % 2
    dz = jnp.asarray(np.array(ring_steps(8), np.int32))
    dx = jnp.asarray(np.array(ring_steps(4), np.int32))
    member = (
        ((z + dz) % 8)[:, None, None] * 8
        + ((x + dx) % 4)[None, :, None] * 2
        + (yl ^ jnp.arange(2, dtype=jnp.int32))[None, None, :]
    ).reshape(GROUPS)
    shard = jnp.arange(SHARDS, dtype=jnp.int32)
    offset = (member[:, None] - shard[None, :]) % 64
    held = jnp.maximum((all_counts[None, :] - offset + 63) // 64, 0)
    before = (shard[:, None] < shard[None, :]).astype(BF)
    start = jnp.dot(held.astype(BF), before, preferred_element_type=F32).astype(jnp.int32)
    base = shard[None, :] * ROWS + offset - 64 * start
    place = jnp.arange(CAP, dtype=jnp.int32)[None, None, :]
    inside = (start[:, :, None] <= place) & (place < (start + held)[:, :, None])
    ids = jnp.sum(jnp.where(inside, base[:, :, None] + 64 * place, 0), axis=1)
    fill = jnp.sum(held, axis=1)
    ids = jnp.where(place[0] < fill[:, None], ids, BIG)

    slot = jnp.arange(SLOTS, dtype=jnp.int32)[None, :]
    pos = jnp.where(slot < held[0][:, None], start[0][:, None] + slot, -1).reshape(-1)
    own_ids = ids[0]
    tiles = own_ids.reshape(NQ, QT)
    dead = tiles >= BIG
    q_max = jnp.max(jnp.where(dead, -1, tiles), axis=1)
    q_min = jnp.min(tiles, axis=1)
    k_group = ids.reshape(GROUPS, NK, KT)
    k_min, k_max = jnp.min(k_group, axis=(0, 2)), jnp.max(k_group, axis=(0, 2))
    n_vis = jnp.sum((k_min[None, :] <= q_max[:, None]).astype(jnp.int32), axis=1)
    n_full = jnp.sum((k_max[None, :] <= q_min[:, None]) & (k_max < BIG)[None, :], axis=1)
    n_full = jnp.minimum(n_full.astype(jnp.int32), n_vis)
    q_ids = jnp.tile(tiles[:, None, :], (1, 4, 1)).reshape(NQ, 4 * QT, 1)
    k_ids = (
        ids.reshape(4, 2, 8, NK, KT).transpose(0, 3, 1, 2, 4).reshape(4, NK, 1, 16 * KT)
    )

    k_own, v_own = pl.pallas_call(
        compact_kernel,
        out_shape=(jax.ShapeDtypeStruct((CAP, 128), BF),) * 2,
        in_specs=[VMEM] * 2,
        out_specs=(VMEM, VMEM),
        compiler_params=params(16),
        name="compact",
    )(pos[None, :], kv_got)

    k_all = jnp.stack([k_own, hop(k_own, "y")])
    k_all = ring(k_all, "x", 4, 1)
    k_all = ring(k_all, "z", 8, 2).reshape(8, 8, CAP, 128)
    v_all = ring(v_own, "z", 8, 0)
    v_all = jnp.stack([v_all, hop(v_all, "y")])
    v_all = ring(v_all, "x", 4, 2).reshape(8, 8, CAP, 128)

    o_packed = pl.pallas_call(
        attend_kernel,
        out_shape=jax.ShapeDtypeStruct((1024, 512), BF),
        in_specs=[SMEM, SMEM] + [VMEM] * 7,
        out_specs=VMEM,
        scratch_shapes=[
            pltpu.VMEM((NQ, 4 * QT, 128), BF),
            pltpu.VMEM((CAP, 512), BF),
            pltpu.VMEM((4 * QT, 1), F32),
            pltpu.VMEM((4 * QT, 256), F32),
        ],
        compiler_params=params(40),
        name="attend",
    )(n_vis, n_full, pos[None, :], pos[:, None], q_ids, k_ids, q_got, k_all, v_all)

    o_got = lax.all_to_all(o_packed, "ctx", 0, 0, tiled=True)
    o_home = pl.pallas_call(
        home_kernel,
        out_shape=jax.ShapeDtypeStruct((ROWS, 1024), BF),
        in_specs=[SMEM, VMEM],
        out_specs=VMEM,
        compiler_params=params(16),
        name="home",
    )(rot, o_got.reshape(32, 2, 16, 512))
    o_other = lax.ppermute(o_home, "head", [(0, 1), (1, 0)])

    live = (jnp.arange(ROWS, dtype=jnp.int32) < counts[0]).astype(jnp.int32)
    cols = 512
    steps = half_w // cols
    return pl.pallas_call(
        project_kernel,
        out_shape=jax.ShapeDtypeStruct((ROWS, half_w), BF),
        grid_spec=pltpu.PrefetchScalarGridSpec(
            num_scalar_prefetch=1,
            grid=(steps,),
            in_specs=[
                pl.BlockSpec((ROWS, 1024), lambda i, h: (0, 0)),
                pl.BlockSpec((ROWS, 1024), lambda i, h: (0, 0)),
                pl.BlockSpec((1024, cols), lambda i, h: (0, h[0] * steps + i)),
                pl.BlockSpec((1024, cols), lambda i, h: (0, i)),
                pl.BlockSpec((ROWS, 1), lambda i, h: (0, 0)),
                pl.BlockSpec((ROWS, 1), lambda i, h: (0, 0)),
            ],
            out_specs=pl.BlockSpec((ROWS, cols), lambda i, h: (0, i)),
        ),
        compiler_params=params(32),
        name="project",
    )(hd.reshape(1), o_home, o_other, weight, w_other, router[:, None], live[:, None])


def solution(mesh):
    return jax.shard_map(
        local,
        mesh=mesh,
        in_specs=(
            P("ctx", "head"),
            P("ctx", "head"),
            P("ctx", "head"),
            P("head", None),
            P("ctx"),
            P("ctx"),
            P("ctx"),
        ),
        out_specs=P("ctx", "head"),
        check_vma=False,
    )
```

```python
import functools

import jax
import jax.numpy as jnp
import numpy as np
from jax import lax
from jax.experimental import pallas as pl
from jax.experimental.pallas import tpu as pltpu
from jax.sharding import PartitionSpec as P

HEAD_WIDTH = 128
THETA = 500000.0
CAP = 320
SLOTS = 8
SHARDS = 128
ROWS = 512
T = 64
N = CAP // T
BIG = float(1 << 30)
LOW = -1e30
EXTRA = 16
BF = jnp.bfloat16
F32 = jnp.float32
SCALE2 = float(1.0 / np.sqrt(128.0) * np.log2(np.e))
VMEM = pl.BlockSpec(memory_space=pltpu.VMEM)
SMEM = pl.BlockSpec(memory_space=pltpu.SMEM)


def params(mib):
    return pltpu.CompilerParams(vmem_limit_bytes=mib * 2**20)


def perm_of(axis, k):
    pairs = []
    for d in range(SHARDS):
        z, x, y = d // 16, d // 4 % 4, d % 4
        if axis == "z":
            z = (z + k) % 8
        elif axis == "x":
            x = (x + k) % 4
        else:
            y = y ^ 1
        pairs.append((d, z * 16 + x * 4 + y))
    return pairs


def hop(a, axis, k=1):
    return lax.ppermute(a, "ctx", perm_of(axis, k))


def ring(a, axis, size, row_dim):
    half = a.shape[row_dim] // 2
    out, up, down = [a], a, a
    for _ in range(size // 2 - 1):
        up, down = hop(up, axis, 1), hop(down, axis, -1)
        out += [up, down]
    lo = hop(lax.slice_in_dim(up, 0, half, axis=row_dim), axis, 1)
    hi = hop(lax.slice_in_dim(down, half, 2 * half, axis=row_dim), axis, -1)
    out.append(jnp.concatenate([lo, hi], axis=row_dim))
    return out


def ring_steps(size):
    steps = [0]
    for i in range(1, size // 2):
        steps += [-i, i]
    return steps + [size // 2]


def pack_matrix(rot, transpose):
    packed_dim = 1 if transpose else 0
    o = lax.broadcasted_iota(jnp.int32, (ROWS, ROWS), packed_dim)
    s = lax.broadcasted_iota(jnp.int32, (ROWS, ROWS), 1 - packed_dim)
    src = (o & 7) * 64 + (((o >> 3) + 64 - rot) & 63)
    return jnp.where(src == s, 1.0, 0.0).astype(BF)


def pack_kernel(rot_ref, count_ref, q_ref, k_ref, v_ref, cos_ref, sin_ref, kv_ref, qp_ref):
    cos, sin = cos_ref[...], sin_ref[...]

    def rotate(x):
        x = x.astype(F32)
        return (x * cos + pltpu.roll(x, 64, 1) * sin).astype(BF)

    m = pack_matrix(rot_ref[0], False)
    lane = lax.broadcasted_iota(jnp.int32, (32, 16, 128), 2)
    count = count_ref[0]
    note = jnp.where(lane == 0, count >> 8, jnp.where(lane == 1, count & 255, 0))
    note = note.astype(F32).astype(BF)
    for h in range(2):
        kv_ref[:, h, :, 256:] = note
        k = rotate(k_ref[:, h * 128 : (h + 1) * 128])
        v = v_ref[:, h * 128 : (h + 1) * 128]
        for c, x in ((0, k), (1, v)):
            y = jnp.dot(m, x, preferred_element_type=F32).astype(BF)
            kv_ref[:, h, :, c * 128 : (c + 1) * 128] = y.reshape(32, 16, 128)
        for g in range(4):
            x = rotate(q_ref[:, h * 512 + g * 128 : h * 512 + (g + 1) * 128])
            y = jnp.dot(m, x, preferred_element_type=F32).astype(BF)
            qp_ref[:, h, :, g * 128 : (g + 1) * 128] = y.reshape(32, 16, 128)


def compact_matrix(pos):
    p = lax.broadcasted_iota(jnp.int32, (CAP, SHARDS * SLOTS), 0)
    return jnp.where(p == pos, 1.0, 0.0).astype(BF)


def compact_kernel(pos_ref, x_ref, out_ref):
    m = compact_matrix(pos_ref[...])
    out_ref[...] = jnp.dot(m, x_ref[:, :256], preferred_element_type=F32).astype(BF)


def queries_kernel(pos_ref, x_ref, out_ref):
    m = compact_matrix(pos_ref[...])
    y = jnp.dot(m, x_ref[...], preferred_element_type=F32).astype(BF)
    for i in range(N):
        for g in range(4):
            out_ref[i, g * T : (g + 1) * T, :] = y[i * T : (i + 1) * T, g * 128 : (g + 1) * 128]


def attend_kernel(slabs, first, last, *refs):
    n = len(slabs)
    nvis_ref, nfull_ref, qid_ref, kid_ref, qa_ref, qb_ref = refs[:6]
    kv_refs, refs = refs[6 : 6 + n], refs[6 + n :]
    if not first:
        refs = refs[2:]
    ml_ref, acc_ref = refs[:2]
    if first:
        row = lax.broadcasted_iota(jnp.int32, ml_ref.shape, 2)
        ml_ref[...] = jnp.where(row == 0, LOW, 0.0)
        acc_ref[...] = jnp.zeros_like(acc_ref)

    def tile(i, _):
        def step(masked, j, _):
            r = pl.multiple_of(j * T, T)
            keys = [kv[:, pl.ds(r, T), :128].reshape(4 * T, 128) for kv in kv_refs]
            vals = [kv[:, pl.ds(r, T), 128:].reshape(4 * T, 128) for kv in kv_refs]
            kids = []
            if masked:
                for d in slabs:
                    col = jnp.broadcast_to(kid_ref[d, j], (128, 4 * T)).T
                    kids.append(jnp.concatenate([col, col], axis=1))
            for half, q_ref in enumerate((qa_ref, qb_ref)):
                q = q_ref[i]
                scores = [
                    lax.dot_general(key, q, (((1,), (1,)), ((), ())), preferred_element_type=F32)
                    for key in keys
                ]
                if masked:
                    qid = qid_ref[half, i]
                    scores = [jnp.where(kid <= qid, s, LOW) for kid, s in zip(kids, scores)]
                old = ml_ref[half, i, 0:1, :]
                new = old
                for s in scores:
                    new = jnp.maximum(new, jnp.max(s, axis=0, keepdims=True))
                keep = jnp.exp2((old - new) * SCALE2)
                total = ml_ref[half, i, 1:2, :] * keep
                acc = acc_ref[half, i] * keep
                for s, val in zip(scores, vals):
                    p = jnp.exp2((s - new) * SCALE2)
                    total = total + jnp.sum(p, axis=0, keepdims=True)
                    acc = acc + lax.dot_general(
                        val, p.astype(BF), (((0,), (0,)), ((), ())), preferred_element_type=F32
                    )
                ml_ref[half, i, 0:1, :] = new
                ml_ref[half, i, 1:2, :] = total
                acc_ref[half, i] = acc
            return 0

        full, vis = nfull_ref[i], nvis_ref[i]
        lax.fori_loop(0, full, functools.partial(step, False), 0)
        lax.fori_loop(full, vis, functools.partial(step, True), 0)
        if last:
            o, lse = finish(ml_ref[1, i], acc_ref[1, i])
            hi = lse.astype(BF).astype(F32)
            mid = (lse - hi).astype(BF).astype(F32)
            lo = lse - hi - mid
            row = lax.broadcasted_iota(jnp.int32, (EXTRA, 4 * T), 0)
            note = jnp.where(row == 0, hi, jnp.where(row == 1, mid, jnp.where(row == 2, lo, 0.0)))
            refs[2][i, :128, :] = o.astype(BF)
            refs[2][i, 128:, :] = note.astype(BF)
        return 0

    lax.fori_loop(0, N, tile, 0)


def finish(ml, acc):
    m, total = ml[0:1], ml[1:2]
    some = total > 0.0
    total = jnp.where(some, total, 1.0)
    lse = jnp.where(some, m * SCALE2 + jnp.log2(total), LOW)
    return acc / total, lse


def merge_kernel(post_ref, ml_ref, acc_ref, got_ref, out_ref, ob_ref):
    for i in range(N):
        mine, lse_a = finish(ml_ref[0, i], acc_ref[0, i])
        got = got_ref[i].astype(F32)
        lse_b = got[128:129] + got[129:130] + got[130:131]
        top = jnp.maximum(lse_a, lse_b)
        wa, wb = jnp.exp2(lse_a - top), jnp.exp2(lse_b - top)
        inv = 1.0 / (wa + wb)
        o = (mine * (wa * inv) + got[:128] * (wb * inv)).T.astype(BF)
        for g in range(4):
            ob_ref[i * T : (i + 1) * T, g * 128 : (g + 1) * 128] = o[g * T : (g + 1) * T]
    p = lax.broadcasted_iota(jnp.int32, (SHARDS * SLOTS, CAP), 1)
    spread = jnp.where(p == post_ref[...], 1.0, 0.0).astype(BF)
    out_ref[...] = jnp.dot(spread, ob_ref[...], preferred_element_type=F32).astype(BF)


def home_kernel(rot_ref, o_ref, out_ref):
    m = pack_matrix(rot_ref[0], True)
    for h in range(2):
        x = o_ref[:, h, :, :].reshape(ROWS, 512)
        out_ref[:, h * 512 : (h + 1) * 512] = jnp.dot(m, x, preferred_element_type=F32).astype(BF)


def project_kernel(hd_ref, own_ref, other_ref, wa_ref, wb_ref, gain_ref, live_ref, out_ref):
    s = jnp.dot(own_ref[...], wa_ref[...], preferred_element_type=F32)
    s = s + jnp.dot(other_ref[...], wb_ref[...], preferred_element_type=F32)
    s = s.astype(BF).astype(F32)
    out_ref[...] = jnp.where(live_ref[...] > 0, gain_ref[...] * s, 0.0).astype(BF)


def local(q_home, k_home, v_home, weight, router, positions, counts):
    d = lax.axis_index("ctx").astype(jnp.int32)
    hd = lax.axis_index("head").astype(jnp.int32)
    half_w = weight.shape[1] // 2

    theirs = lax.dynamic_slice_in_dim(weight, (1 - hd) * half_w, half_w, axis=1)
    w_other = lax.ppermute(theirs, "head", [(0, 1), (1, 0)])

    freqs = THETA ** (-(jnp.arange(64, dtype=F32) * 2.0 / HEAD_WIDTH))
    angles = positions.astype(F32)[:, None] * jnp.concatenate([freqs, freqs])[None, :]
    sign = jnp.where(jnp.arange(128) < 64, -1.0, 1.0).astype(F32)
    cos, sin = jnp.cos(angles), jnp.sin(angles) * sign[None, :]
    rot = (d % 64).reshape(1)

    kv_packed, q_packed = pl.pallas_call(
        pack_kernel,
        out_shape=(
            jax.ShapeDtypeStruct((32, 2, 16, 384), BF),
            jax.ShapeDtypeStruct((32, 2, 16, 512), BF),
        ),
        in_specs=[SMEM] * 2 + [VMEM] * 5,
        out_specs=(VMEM, VMEM),
        compiler_params=params(32),
        name="pack",
    )(rot, counts, q_home, k_home, v_home, cos, sin)
    kv_got = lax.all_to_all(kv_packed.reshape(1024, 384), "ctx", 0, 0, tiled=True)
    note = kv_got.reshape(SHARDS, SLOTS, 384)[:, 0, 256:258].astype(jnp.int32)
    all_counts = note[:, 0] * 256 + note[:, 1]

    z, x, yl = d // 16, d // 4 % 4, d % 2
    dz = jnp.asarray(np.array(ring_steps(8), np.int32))
    dx = jnp.asarray(np.array(ring_steps(4), np.int32))
    member = ((z + dz) % 8)[:, None] * 8 + ((x + dx) % 4)[None, :] * 2 + yl
    partner = z * 8 + x * 2 + (1 - yl)
    member = jnp.concatenate([member.reshape(32), partner.reshape(1)])
    shard = jnp.arange(SHARDS, dtype=jnp.int32)

    def layout(who):
        offset = (who[:, None] - shard[None, :]) % 64
        held = jnp.maximum((all_counts[None, :] - offset + 63) // 64, 0)
        before = (shard[:, None] < shard[None, :]).astype(BF)
        start = jnp.dot(held.astype(BF), before, preferred_element_type=F32).astype(jnp.int32)
        return offset, held, start

    _, held, start = layout(member[:1])
    slot = jnp.arange(SLOTS, dtype=jnp.int32)[None, :]
    pos = jnp.where(slot < held[0][:, None], start[0][:, None] + slot, -1).reshape(-1)
    kv_own = pl.pallas_call(
        compact_kernel,
        out_shape=jax.ShapeDtypeStruct((CAP, 256), BF),
        in_specs=[VMEM] * 2,
        out_specs=VMEM,
        compiler_params=params(16),
        name="compact",
    )(pos[None, :], kv_got)
    q_got = lax.all_to_all(q_packed.reshape(1024, 512), "ctx", 0, 0, tiled=True)
    q_own = pl.pallas_call(
        queries_kernel,
        out_shape=jax.ShapeDtypeStruct((N, 4 * T, 128), BF),
        in_specs=[VMEM] * 2,
        out_specs=VMEM,
        compiler_params=params(16),
        name="queries",
    )(pos[None, :], q_got)
    q_partner = hop(q_own, "y")

    offset, held, start = layout(member)
    base = (shard[None, :] * ROWS + offset - 64 * start).astype(F32)
    place = jnp.arange(CAP, dtype=jnp.int32)[None, None, :]
    inside = (start[:, :, None] <= place) & (place < (start + held)[:, :, None])
    ids = jnp.sum(jnp.where(inside, base[:, :, None] + (64 * place).astype(F32), 0.0), axis=1)
    ids = jnp.where(place[0] < jnp.sum(held, axis=1)[:, None], ids, BIG)
    q_tiles = jnp.stack([ids[0], ids[32]]).reshape(2, N, T)
    q_max = jnp.max(jnp.where(q_tiles >= BIG, -1.0, q_tiles), axis=(0, 2))
    q_min = jnp.min(q_tiles, axis=(0, 2))
    slabs_ids = ids[:32].reshape(8, 4, N, T)
    k_min, k_max = jnp.min(slabs_ids, axis=(1, 3)), jnp.max(slabs_ids, axis=(1, 3))
    sees = k_min[:, None, :] <= q_max[None, :, None]
    whole = (k_max[:, None, :] <= q_min[None, :, None]) & (k_max < BIG)[:, None, :]
    q_ids = jnp.tile(q_tiles[:, :, None, :], (1, 1, 1, 4))
    k_ids = slabs_ids.transpose(0, 2, 1, 3).reshape(8, N, 1, 4 * T)

    slab = jnp.stack(ring(kv_own, "x", 4, 0))
    slabs = ring(slab, "z", 8, 1)
    state = ()
    chunks = ((0,), (1, 2), (3, 4), (5, 6), (7,))
    for c, chunk in enumerate(chunks):
        first, last, n = c == 0, c == len(chunks) - 1, len(chunk)
        n_vis = jnp.sum(jnp.any(sees[chunk[0] : chunk[-1] + 1], axis=0), axis=1).astype(jnp.int32)
        n_full = jnp.sum(jnp.all(whole[chunk[0] : chunk[-1] + 1], axis=0), axis=1).astype(jnp.int32)
        n_full = jnp.minimum(n_full, n_vis)
        shapes = [
            jax.ShapeDtypeStruct((2, N, 8, 4 * T), F32),
            jax.ShapeDtypeStruct((2, N, 128, 4 * T), F32),
        ]
        if last:
            shapes.append(jax.ShapeDtypeStruct((N, 128 + EXTRA, 4 * T), BF))
        state = pl.pallas_call(
            functools.partial(attend_kernel, chunk, first, last),
            out_shape=tuple(shapes),
            in_specs=[SMEM] * 2 + [VMEM] * (4 + n + len(state)),
            out_specs=(VMEM,) * len(shapes),
            input_output_aliases={} if first else {6 + n: 0, 7 + n: 1},
            compiler_params=params(24),
            cost_estimate=pl.CostEstimate(
                flops=n * 2_000_000_000, bytes_accessed=n * 4_000_000, transcendentals=n * 2_000_000
            ),
            name="attend",
        )(n_vis, n_full, q_ids, k_ids, q_own, q_partner, *[slabs[k] for k in chunk], *state)
    ml, acc, message = state
    got = hop(message, "y")

    o_packed = pl.pallas_call(
        merge_kernel,
        out_shape=jax.ShapeDtypeStruct((1024, 512), BF),
        in_specs=[VMEM] * 4,
        out_specs=VMEM,
        scratch_shapes=[pltpu.VMEM((CAP, 512), BF)],
        compiler_params=params(24),
        name="merge",
    )(pos[:, None], ml, acc, got)

    o_got = lax.all_to_all(o_packed, "ctx", 0, 0, tiled=True)
    o_home = pl.pallas_call(
        home_kernel,
        out_shape=jax.ShapeDtypeStruct((ROWS, 1024), BF),
        in_specs=[SMEM, VMEM],
        out_specs=VMEM,
        compiler_params=params(16),
        name="home",
    )(rot, o_got.reshape(32, 2, 16, 512))
    o_other = lax.ppermute(o_home, "head", [(0, 1), (1, 0)])

    live = (jnp.arange(ROWS, dtype=jnp.int32) < counts[0]).astype(jnp.int32)
    cols = 512
    steps = half_w // cols
    return pl.pallas_call(
        project_kernel,
        out_shape=jax.ShapeDtypeStruct((ROWS, half_w), BF),
        grid_spec=pltpu.PrefetchScalarGridSpec(
            num_scalar_prefetch=1,
            grid=(steps,),
            in_specs=[
                pl.BlockSpec((ROWS, 1024), lambda i, h: (0, 0)),
                pl.BlockSpec((ROWS, 1024), lambda i, h: (0, 0)),
                pl.BlockSpec((1024, cols), lambda i, h: (0, h[0] * steps + i)),
                pl.BlockSpec((1024, cols), lambda i, h: (0, i)),
                pl.BlockSpec((ROWS, 1), lambda i, h: (0, 0)),
                pl.BlockSpec((ROWS, 1), lambda i, h: (0, 0)),
            ],
            out_specs=pl.BlockSpec((ROWS, cols), lambda i, h: (0, i)),
        ),
        compiler_params=params(32),
        name="project",
    )(hd.reshape(1), o_home, o_other, weight, w_other, router[:, None], live[:, None])


def solution(mesh):
    return jax.shard_map(
        local,
        mesh=mesh,
        in_specs=(
            P("ctx", "head"),
            P("ctx", "head"),
            P("ctx", "head"),
            P("head", None),
            P("ctx"),
            P("ctx"),
            P("ctx"),
        ),
        out_specs=P("ctx", "head"),
        check_vma=False,
    )
```

```python
import functools

import jax
import jax.numpy as jnp
import numpy as np
from jax import lax
from jax.experimental import pallas as pl
from jax.experimental.pallas import tpu as pltpu
from jax.sharding import PartitionSpec as P

HEAD_WIDTH = 128
THETA = 500000.0
CAP = 320
SLOTS = 8
SHARDS = 128
ROWS = 512
T = 64
N = CAP // T
TILES = N + 1
REACH = (80, 144, 208, 272, 272, 272)
MORE = 16
BIG = float(1 << 30)
LOW = -1e30
EXTRA = 16
BF = jnp.bfloat16
F32 = jnp.float32
SCALE2 = float(1.0 / np.sqrt(128.0) * np.log2(np.e))
VMEM = pl.BlockSpec(memory_space=pltpu.VMEM)
SMEM = pl.BlockSpec(memory_space=pltpu.SMEM)


def params(mib):
    return pltpu.CompilerParams(vmem_limit_bytes=mib * 2**20)


def perm_of(axis, k):
    pairs = []
    for d in range(SHARDS):
        z, x, y = d // 16, d // 4 % 4, d % 4
        if axis == "z":
            z = (z + k) % 8
        elif axis == "x":
            x = (x + k) % 4
        else:
            y = y ^ 1
        pairs.append((d, z * 16 + x * 4 + y))
    return pairs


def hop(a, axis, k=1):
    return lax.ppermute(a, "ctx", perm_of(axis, k))


def ring(a, axis, size, row_dim):
    half = a.shape[row_dim] // 2
    out, up, down = [a], a, a
    for _ in range(size // 2 - 1):
        up, down = hop(up, axis, 1), hop(down, axis, -1)
        out += [up, down]
    lo = hop(lax.slice_in_dim(up, 0, half, axis=row_dim), axis, 1)
    hi = hop(lax.slice_in_dim(down, half, 2 * half, axis=row_dim), axis, -1)
    out.append(jnp.concatenate([lo, hi], axis=row_dim))
    return out


def ring_steps(size):
    steps = [0]
    for i in range(1, size // 2):
        steps += [-i, i]
    return steps + [size // 2]


def pack_matrix(rot, transpose):
    packed_dim = 1 if transpose else 0
    o = lax.broadcasted_iota(jnp.int32, (ROWS, ROWS), packed_dim)
    s = lax.broadcasted_iota(jnp.int32, (ROWS, ROWS), 1 - packed_dim)
    src = (o & 7) * 64 + (((o >> 3) + 64 - rot) & 63)
    return jnp.where(src == s, 1.0, 0.0).astype(BF)


def pack_kernel(rot_ref, q_ref, k_ref, v_ref, cos_ref, sin_ref, out_ref):
    cos, sin = cos_ref[...], sin_ref[...]

    def rotate(x):
        x = x.astype(F32)
        return (x * cos + pltpu.roll(x, 64, 1) * sin).astype(BF)

    m = pack_matrix(rot_ref[0], False)
    for h in range(2):
        parts = [rotate(q_ref[:, h * 512 + g * 128 : h * 512 + (g + 1) * 128]) for g in range(4)]
        parts.append(rotate(k_ref[:, h * 128 : (h + 1) * 128]))
        parts.append(v_ref[:, h * 128 : (h + 1) * 128])
        for c, x in enumerate(parts):
            y = jnp.dot(m, x, preferred_element_type=F32).astype(BF)
            out_ref[:, h, :, c * 128 : (c + 1) * 128] = y.reshape(32, 16, 128)


def compact_matrix(pos):
    p = lax.broadcasted_iota(jnp.int32, (CAP, SHARDS * SLOTS), 0)
    return jnp.where(p == pos, 1.0, 0.0).astype(BF)


def columns(i):
    if i < N - 1:
        return [(i * T, T, g) for g in range(4)]
    return [(i * T + b * 32, 32, g) for b in range(2) for g in range(4)]


def compact_kernel(pos_ref, x_ref, kv_ref, q_ref):
    m = compact_matrix(pos_ref[...])
    kv_ref[...] = jnp.dot(m, x_ref[:, 512:], preferred_element_type=F32).astype(BF)
    y = jnp.dot(m, x_ref[:, :512], preferred_element_type=F32).astype(BF)
    for i in range(N):
        at = 0
        for row, rows, g in columns(i):
            q_ref[i, at : at + rows, :] = y[row : row + rows, g * 128 : (g + 1) * 128]
            at += rows


def attend_kernel(n, first, last, *refs):
    more_ref, live_ref, qid_ref, kid_ref, qa_ref, qb_ref = refs[:6]
    kv_refs, refs = refs[6 : 6 + n], refs[6 + n :]
    if not first:
        refs = refs[2:]
    ml_ref, acc_ref = refs[:2]
    if first:
        row = lax.broadcasted_iota(jnp.int32, ml_ref.shape, 2)
        ml_ref[...] = jnp.where(row == 0, LOW, 0.0)
        acc_ref[...] = jnp.zeros_like(acc_ref)

    def batch(tiles, start, rows):
        at = pl.ds(start, rows)
        keys = [kv[:, at, :128].reshape(4 * rows, 128) for kv in kv_refs]
        vals = [kv[:, at, 128:].reshape(4 * rows, 128) for kv in kv_refs]
        kids = []
        for c in range(n):
            col = kid_ref[c, :, at, :].reshape(4 * rows, 128)
            kids.append(jnp.concatenate([col, col], axis=1))
        old = [(ml_ref[h, i, 0:1, :], ml_ref[h, i, 1:2, :], acc_ref[h, i]) for _, _, h, i in tiles]
        found = []
        for (q, qid, _, _), (m, _, _) in zip(tiles, old):
            scores = []
            for key, kid in zip(keys, kids):
                s = lax.dot_general(key, q, (((1,), (1,)), ((), ())), preferred_element_type=F32)
                s = jnp.where(kid <= qid, s, LOW)
                m = jnp.maximum(m, jnp.max(s, axis=0, keepdims=True))
                scores.append(s)
            found.append((scores, m))
        done = []
        for (scores, new), (m, total, acc) in zip(found, old):
            keep = jnp.exp2((m - new) * SCALE2)
            total, acc = total * keep, acc * keep
            for s, val in zip(scores, vals):
                p = jnp.exp2((s - new) * SCALE2)
                total = total + jnp.sum(p, axis=0, keepdims=True)
                acc = acc + lax.dot_general(
                    val, p.astype(BF), (((0,), (0,)), ((), ())), preferred_element_type=F32
                )
            done.append((new, total, acc))
        for (_, _, h, i), (m, total, acc) in zip(tiles, done):
            ml_ref[h, i, 0:1, :] = m
            ml_ref[h, i, 1:2, :] = total
            acc_ref[h, i] = acc

    def visit(i):
        if i < N - 1:
            tiles = [(qa_ref[i], qid_ref[0, i], 0, i), (qb_ref[i], qid_ref[1, i], 1, i)]
        else:
            b = i - (N - 1)
            c = slice(b * 128, (b + 1) * 128)
            q = jnp.concatenate([qa_ref[N - 1, c], qb_ref[N - 1, c]], axis=0)
            qid = jnp.concatenate([qid_ref[0, N - 1, :, c], qid_ref[1, N - 1, :, c]], axis=1)
            tiles = [(q, qid, b, N - 1)]
        batch(tiles, 0, REACH[i])

        def further(e, _):
            batch(tiles, pl.multiple_of(REACH[i] + e * MORE, MORE), MORE)
            return 0

        lax.fori_loop(0, more_ref[i], further, 0)

    for i in range(TILES):
        if i < N - 1:
            visit(i)
        else:
            pl.when(live_ref[i] > 0)(functools.partial(visit, i))
    if last:
        for i in range(N):
            o, lse = of_half(1, i, ml_ref, acc_ref)
            hi = lse.astype(BF).astype(F32)
            mid = (lse - hi).astype(BF).astype(F32)
            lo = lse - hi - mid
            row = lax.broadcasted_iota(jnp.int32, (EXTRA, 4 * T), 0)
            note = jnp.where(row == 0, hi, jnp.where(row == 1, mid, jnp.where(row == 2, lo, 0.0)))
            refs[2][i, :128, :] = o.astype(BF)
            refs[2][i, 128:, :] = note.astype(BF)


def of_half(half, i, ml_ref, acc_ref):
    if i < N - 1:
        return finish(ml_ref[half, i], acc_ref[half, i])
    c = slice(half * 128, (half + 1) * 128)
    ml = jnp.concatenate([ml_ref[0, i, :, c], ml_ref[1, i, :, c]], axis=1)
    acc = jnp.concatenate([acc_ref[0, i, :, c], acc_ref[1, i, :, c]], axis=1)
    return finish(ml, acc)


def finish(ml, acc):
    m, total = ml[0:1], ml[1:2]
    some = total > 0.0
    total = jnp.where(some, total, 1.0)
    lse = jnp.where(some, m * SCALE2 + jnp.log2(total), LOW)
    return acc / total, lse


def merge_kernel(post_ref, ml_ref, acc_ref, got_ref, out_ref, ob_ref):
    for i in range(N):
        mine, lse_a = of_half(0, i, ml_ref, acc_ref)
        got = got_ref[i].astype(F32)
        lse_b = got[128:129] + got[129:130] + got[130:131]
        top = jnp.maximum(lse_a, lse_b)
        wa, wb = jnp.exp2(lse_a - top), jnp.exp2(lse_b - top)
        inv = 1.0 / (wa + wb)
        o = (mine * (wa * inv) + got[:128] * (wb * inv)).T.astype(BF)
        at = 0
        for row, rows, g in columns(i):
            ob_ref[row : row + rows, g * 128 : (g + 1) * 128] = o[at : at + rows]
            at += rows
    p = lax.broadcasted_iota(jnp.int32, (SHARDS * SLOTS, CAP), 1)
    spread = jnp.where(p == post_ref[...], 1.0, 0.0).astype(BF)
    out_ref[...] = jnp.dot(spread, ob_ref[...], preferred_element_type=F32).astype(BF)


def home_kernel(rot_ref, o_ref, out_ref):
    m = pack_matrix(rot_ref[0], True)
    for h in range(2):
        x = o_ref[:, h, :, :].reshape(ROWS, 512)
        out_ref[:, h * 512 : (h + 1) * 512] = jnp.dot(m, x, preferred_element_type=F32).astype(BF)


def project_kernel(hd_ref, own_ref, other_ref, wa_ref, wb_ref, gain_ref, live_ref, out_ref):
    s = jnp.dot(own_ref[...], wa_ref[...], preferred_element_type=F32)
    s = s + jnp.dot(other_ref[...], wb_ref[...], preferred_element_type=F32)
    s = s.astype(BF).astype(F32)
    out_ref[...] = jnp.where(live_ref[...] > 0, gain_ref[...] * s, 0.0).astype(BF)


def local(q_home, k_home, v_home, weight, router, positions, counts):
    d = lax.axis_index("ctx").astype(jnp.int32)
    hd = lax.axis_index("head").astype(jnp.int32)
    half_w = weight.shape[1] // 2

    to_send = lax.dynamic_slice_in_dim(weight, (1 - hd) * half_w, half_w, axis=1)
    w_other = lax.ppermute(to_send, "head", [(0, 1), (1, 0)])

    freqs = THETA ** (-(jnp.arange(64, dtype=F32) * 2.0 / HEAD_WIDTH))
    angles = positions.astype(F32)[:, None] * jnp.concatenate([freqs, freqs])[None, :]
    sign = jnp.where(jnp.arange(128) < 64, -1.0, 1.0).astype(F32)
    cos, sin = jnp.cos(angles), jnp.sin(angles) * sign[None, :]
    rot = (d % 64).reshape(1)

    packed = pl.pallas_call(
        pack_kernel,
        out_shape=jax.ShapeDtypeStruct((32, 2, 16, 768), BF),
        in_specs=[SMEM] + [VMEM] * 5,
        out_specs=VMEM,
        compiler_params=params(32),
        name="pack",
    )(rot, q_home, k_home, v_home, cos, sin)
    got = lax.all_to_all(packed.reshape(1024, 768), "ctx", 0, 0, tiled=True)
    all_counts = lax.all_gather(counts, "ctx", axis=0, tiled=True)

    z, x, yl = d // 16, d // 4 % 4, d % 2
    dz = jnp.asarray(np.array(ring_steps(8), np.int32))
    dx = jnp.asarray(np.array(ring_steps(4), np.int32))
    member = ((z + dz) % 8)[:, None] * 8 + ((x + dx) % 4)[None, :] * 2 + yl
    partner = z * 8 + x * 2 + (1 - yl)
    member = jnp.concatenate([member.reshape(32), partner.reshape(1)])
    shard = jnp.arange(SHARDS, dtype=jnp.int32)

    def layout(who):
        offset = (who[:, None] - shard[None, :]) % 64
        held = jnp.maximum((all_counts[None, :] - offset + 63) // 64, 0)
        before = (shard[:, None] < shard[None, :]).astype(BF)
        start = jnp.dot(held.astype(BF), before, preferred_element_type=F32).astype(jnp.int32)
        return offset, held, start

    _, held, start = layout(member[:1])
    slot = jnp.arange(SLOTS, dtype=jnp.int32)[None, :]
    pos = jnp.where(slot < held[0][:, None], start[0][:, None] + slot, -1).reshape(-1)
    kv_own, q_own = pl.pallas_call(
        compact_kernel,
        out_shape=(
            jax.ShapeDtypeStruct((CAP, 256), BF),
            jax.ShapeDtypeStruct((N, 4 * T, 128), BF),
        ),
        in_specs=[VMEM] * 2,
        out_specs=(VMEM, VMEM),
        compiler_params=params(16),
        name="compact",
    )(pos[None, :], got)
    q_partner = hop(q_own, "y")

    offset, held, start = layout(member)
    base = (shard[None, :] * ROWS + offset - 64 * start).astype(F32)
    place = jnp.arange(CAP, dtype=jnp.int32)[None, None, :]
    inside = (start[:, :, None] <= place) & (place < (start + held)[:, :, None])
    ids = jnp.sum(jnp.where(inside, base[:, :, None] + (64 * place).astype(F32), 0.0), axis=1)
    ids = jnp.where(place[0] < jnp.sum(held, axis=1)[:, None], ids, BIG)
    q_rows = jnp.stack([ids[0], ids[32]])
    best = jnp.max(jnp.where(q_rows >= BIG, -1.0, q_rows), axis=0)
    edges = [i * T for i in range(N)] + [CAP - 32, CAP]
    q_max = jnp.stack([jnp.max(best[a:b]) for a, b in zip(edges, edges[1:])])
    live = (q_max >= 0.0).astype(jnp.int32)
    reach = jnp.sum((ids[:32, None, :] <= q_max[None, :, None]).astype(jnp.int32), axis=2)
    reach = jnp.max(reach.reshape(8, 4, TILES), axis=1)
    more = jnp.maximum(reach - jnp.asarray(REACH, jnp.int32)[None, :] + MORE - 1, 0) // MORE
    q_tiles = q_rows[:, : CAP - T].reshape(2, N - 1, 1, T)
    q_ids = jnp.tile(q_tiles[:, :, :, :], (1, 1, 4, 1)).reshape(2, N - 1, 1, 4 * T)
    q_last = jnp.tile(q_rows[:, CAP - T :].reshape(2, 2, 1, 32), (1, 1, 4, 1))
    q_ids = jnp.concatenate([q_ids, q_last.reshape(2, 1, 1, 4 * T)], axis=1)
    slab_ids = ids[:32].reshape(8, 4, CAP, 1)

    slab = jnp.stack(ring(kv_own, "x", 4, 0))
    slab, q_partner = lax.optimization_barrier((slab, q_partner))
    slabs = ring(slab, "z", 8, 1)
    state = ()
    chunks = ((0,), (1, 2), (3, 4), (5, 6), (7,))
    for c, chunk in enumerate(chunks):
        first, last, n = c == 0, c == len(chunks) - 1, len(chunk)
        steps = jnp.max(more[chunk[0] : chunk[-1] + 1], axis=0)
        k_ids = jnp.broadcast_to(slab_ids[chunk[0] : chunk[-1] + 1], (n, 4, CAP, 128))
        shapes = [
            jax.ShapeDtypeStruct((2, N, 8, 4 * T), F32),
            jax.ShapeDtypeStruct((2, N, 128, 4 * T), F32),
        ]
        if last:
            shapes.append(jax.ShapeDtypeStruct((N, 128 + EXTRA, 4 * T), BF))
        state = pl.pallas_call(
            functools.partial(attend_kernel, n, first, last),
            out_shape=tuple(shapes),
            in_specs=[SMEM] * 2 + [VMEM] * (4 + n + len(state)),
            out_specs=(VMEM,) * len(shapes),
            input_output_aliases={} if first else {6 + n: 0, 7 + n: 1},
            compiler_params=params(48),
            cost_estimate=pl.CostEstimate(
                flops=n * 4_000_000_000, bytes_accessed=n * 4_000_000, transcendentals=n * 2_000_000
            ),
            name="attend",
        )(steps, live, q_ids, k_ids, q_own, q_partner, *[slabs[k] for k in chunk], *state)
    ml, acc, message = state
    theirs = hop(message, "y")

    o_packed = pl.pallas_call(
        merge_kernel,
        out_shape=jax.ShapeDtypeStruct((1024, 512), BF),
        in_specs=[VMEM] * 4,
        out_specs=VMEM,
        scratch_shapes=[pltpu.VMEM((CAP, 512), BF)],
        compiler_params=params(24),
        name="merge",
    )(pos[:, None], ml, acc, theirs)

    o_got = lax.all_to_all(o_packed, "ctx", 0, 0, tiled=True)
    o_home = pl.pallas_call(
        home_kernel,
        out_shape=jax.ShapeDtypeStruct((ROWS, 1024), BF),
        in_specs=[SMEM, VMEM],
        out_specs=VMEM,
        compiler_params=params(16),
        name="home",
    )(rot, o_got.reshape(32, 2, 16, 512))
    o_other = lax.ppermute(o_home, "head", [(0, 1), (1, 0)])

    live = (jnp.arange(ROWS, dtype=jnp.int32) < counts[0]).astype(jnp.int32)
    cols = 512
    steps = half_w // cols
    return pl.pallas_call(
        project_kernel,
        out_shape=jax.ShapeDtypeStruct((ROWS, half_w), BF),
        grid_spec=pltpu.PrefetchScalarGridSpec(
            num_scalar_prefetch=1,
            grid=(steps,),
            in_specs=[
                pl.BlockSpec((ROWS, 1024), lambda i, h: (0, 0)),
                pl.BlockSpec((ROWS, 1024), lambda i, h: (0, 0)),
                pl.BlockSpec((1024, cols), lambda i, h: (0, h[0] * steps + i)),
                pl.BlockSpec((1024, cols), lambda i, h: (0, i)),
                pl.BlockSpec((ROWS, 1), lambda i, h: (0, 0)),
                pl.BlockSpec((ROWS, 1), lambda i, h: (0, 0)),
            ],
            out_specs=pl.BlockSpec((ROWS, cols), lambda i, h: (0, i)),
        ),
        compiler_params=params(32),
        name="project",
    )(hd.reshape(1), o_home, o_other, weight, w_other, router[:, None], live[:, None])


def solution(mesh):
    return jax.shard_map(
        local,
        mesh=mesh,
        in_specs=(
            P("ctx", "head"),
            P("ctx", "head"),
            P("ctx", "head"),
            P("head", None),
            P("ctx"),
            P("ctx"),
            P("ctx"),
        ),
        out_specs=P("ctx", "head"),
        check_vma=False,
    )
```

```python
import functools

import jax
import jax.numpy as jnp
import numpy as np
from jax import lax
from jax.experimental import pallas as pl
from jax.experimental.pallas import tpu as pltpu
from jax.sharding import PartitionSpec as P

HEAD_WIDTH = 128
THETA = 500000.0
CAP = 320
SLOTS = 8
SHARDS = 128
ROWS = 512
T = 64
N = CAP // T
TILES = N + 1
REACH = (80, 144, 208, 272, 272, 272)
MORE = 16
USUAL = 272
BIG = float(1 << 30)
LOW = -1e30
EXTRA = 16
BF = jnp.bfloat16
F32 = jnp.float32
SCALE2 = float(1.0 / np.sqrt(128.0) * np.log2(np.e))
VMEM = pl.BlockSpec(memory_space=pltpu.VMEM)
SMEM = pl.BlockSpec(memory_space=pltpu.SMEM)


def params(mib):
    return pltpu.CompilerParams(vmem_limit_bytes=mib * 2**20)


def perm_of(axis, k):
    pairs = []
    for d in range(SHARDS):
        z, x, y = d // 16, d // 4 % 4, d % 4
        if axis == "z":
            z = (z + k) % 8
        elif axis == "x":
            x = (x + k) % 4
        else:
            y = y ^ 1
        pairs.append((d, z * 16 + x * 4 + y))
    return pairs


def hop(a, axis, k=1):
    return lax.ppermute(a, "ctx", perm_of(axis, k))


def ring(a, axis, size, row_dim):
    half = a.shape[row_dim] // 2
    out, up, down = [a], a, a
    for _ in range(size // 2 - 1):
        up, down = hop(up, axis, 1), hop(down, axis, -1)
        out += [up, down]
    lo = hop(lax.slice_in_dim(up, 0, half, axis=row_dim), axis, 1)
    hi = hop(lax.slice_in_dim(down, half, 2 * half, axis=row_dim), axis, -1)
    out.append(jnp.concatenate([lo, hi], axis=row_dim))
    return out


def ring_steps(size):
    steps = [0]
    for i in range(1, size // 2):
        steps += [-i, i]
    return steps + [size // 2]


def pack_matrix(rot, transpose):
    packed_dim = 1 if transpose else 0
    o = lax.broadcasted_iota(jnp.int32, (ROWS, ROWS), packed_dim)
    s = lax.broadcasted_iota(jnp.int32, (ROWS, ROWS), 1 - packed_dim)
    src = (o & 7) * 64 + (((o >> 3) + 64 - rot) & 63)
    return jnp.where(src == s, 1.0, 0.0).astype(BF)


def pack_kernel(rot_ref, q_ref, k_ref, v_ref, cos_ref, sin_ref, out_ref):
    cos, sin = cos_ref[...], sin_ref[...]

    def rotate(x):
        x = x.astype(F32)
        return (x * cos + pltpu.roll(x, 64, 1) * sin).astype(BF)

    m = pack_matrix(rot_ref[0], False)
    for h in range(2):
        parts = [rotate(q_ref[:, h * 512 + g * 128 : h * 512 + (g + 1) * 128]) for g in range(4)]
        parts.append(rotate(k_ref[:, h * 128 : (h + 1) * 128]))
        parts.append(v_ref[:, h * 128 : (h + 1) * 128])
        for c, x in enumerate(parts):
            y = jnp.dot(m, x, preferred_element_type=F32).astype(BF)
            out_ref[:, h, :, c * 128 : (c + 1) * 128] = y.reshape(32, 16, 128)


def compact_matrix(pos):
    p = lax.broadcasted_iota(jnp.int32, (CAP, SHARDS * SLOTS), 0)
    return jnp.where(p == pos, 1.0, 0.0).astype(BF)


def columns(i):
    if i < N - 1:
        return [(i * T, T, g) for g in range(4)]
    return [(i * T + b * 32, 32, g) for b in range(2) for g in range(4)]


def compact_kernel(pos_ref, x_ref, kv_ref, q_ref):
    m = compact_matrix(pos_ref[...])
    kv = jnp.dot(m, x_ref[:, 512:], preferred_element_type=F32).astype(BF)
    kv_ref[...] = kv[: kv_ref.shape[0]]
    y = jnp.dot(m, x_ref[:, :512], preferred_element_type=F32).astype(BF)
    for i in range(N):
        at = 0
        for row, rows, g in columns(i):
            q_ref[i, at : at + rows, :] = y[row : row + rows, g * 128 : (g + 1) * 128]
            at += rows


def attend_kernel(n, first, last, *refs):
    more_ref, live_ref, qid_ref, kid_ref, qa_ref, qb_ref = refs[:6]
    kv_refs, refs = refs[6 : 6 + n], refs[6 + n :]
    if not first:
        refs = refs[2:]
    ml_ref, acc_ref = refs[:2]
    if first:
        row = lax.broadcasted_iota(jnp.int32, ml_ref.shape, 2)
        ml_ref[...] = jnp.where(row == 0, LOW, 0.0)
        acc_ref[...] = jnp.zeros_like(acc_ref)

    def batch(tiles, start, rows):
        at = pl.ds(start, rows)
        keys = [kv[:, at, :128].reshape(4 * rows, 128) for kv in kv_refs]
        vals = [kv[:, at, 128:].reshape(4 * rows, 128) for kv in kv_refs]
        kids = []
        for c in range(n):
            col = kid_ref[c, :, at, :].reshape(4 * rows, 128)
            kids.append(jnp.concatenate([col, col], axis=1))
        old = [(ml_ref[h, i, 0:1, :], ml_ref[h, i, 1:2, :], acc_ref[h, i]) for _, _, h, i in tiles]
        found = []
        for (q, qid, _, _), (m, _, _) in zip(tiles, old):
            scores = []
            for key, kid in zip(keys, kids):
                s = lax.dot_general(key, q, (((1,), (1,)), ((), ())), preferred_element_type=F32)
                s = jnp.where(kid <= qid, s, LOW)
                m = jnp.maximum(m, jnp.max(s, axis=0, keepdims=True))
                scores.append(s)
            found.append((scores, m))
        done = []
        for (scores, new), (m, total, acc) in zip(found, old):
            keep = jnp.exp2((m - new) * SCALE2)
            total, acc = total * keep, acc * keep
            for s, val in zip(scores, vals):
                p = jnp.exp2((s - new) * SCALE2)
                total = total + jnp.sum(p, axis=0, keepdims=True)
                acc = acc + lax.dot_general(
                    val, p.astype(BF), (((0,), (0,)), ((), ())), preferred_element_type=F32
                )
            done.append((new, total, acc))
        for (_, _, h, i), (m, total, acc) in zip(tiles, done):
            ml_ref[h, i, 0:1, :] = m
            ml_ref[h, i, 1:2, :] = total
            acc_ref[h, i] = acc

    def visit(i):
        if i < N - 1:
            tiles = [(qa_ref[i], qid_ref[0, i], 0, i), (qb_ref[i], qid_ref[1, i], 1, i)]
        else:
            b = i - (N - 1)
            c = slice(b * 128, (b + 1) * 128)
            q = jnp.concatenate([qa_ref[N - 1, c], qb_ref[N - 1, c]], axis=0)
            qid = jnp.concatenate([qid_ref[0, N - 1, :, c], qid_ref[1, N - 1, :, c]], axis=1)
            tiles = [(q, qid, b, N - 1)]
        batch(tiles, 0, REACH[i])

        def further(e, _):
            batch(tiles, pl.multiple_of(REACH[i] + e * MORE, MORE), MORE)
            return 0

        lax.fori_loop(0, more_ref[i], further, 0)

    for i in range(TILES):
        if i < N - 1:
            visit(i)
        else:
            pl.when(live_ref[i] > 0)(functools.partial(visit, i))
    if last:
        for i in range(N):
            o, lse = of_half(1, i, ml_ref, acc_ref)
            hi = lse.astype(BF).astype(F32)
            mid = (lse - hi).astype(BF).astype(F32)
            lo = lse - hi - mid
            row = lax.broadcasted_iota(jnp.int32, (EXTRA, 4 * T), 0)
            note = jnp.where(row == 0, hi, jnp.where(row == 1, mid, jnp.where(row == 2, lo, 0.0)))
            refs[2][i, :128, :] = o.astype(BF)
            refs[2][i, 128:, :] = note.astype(BF)


def of_half(half, i, ml_ref, acc_ref):
    if i < N - 1:
        return finish(ml_ref[half, i], acc_ref[half, i])
    c = slice(half * 128, (half + 1) * 128)
    ml = jnp.concatenate([ml_ref[0, i, :, c], ml_ref[1, i, :, c]], axis=1)
    acc = jnp.concatenate([acc_ref[0, i, :, c], acc_ref[1, i, :, c]], axis=1)
    return finish(ml, acc)


def finish(ml, acc):
    m, total = ml[0:1], ml[1:2]
    some = total > 0.0
    total = jnp.where(some, total, 1.0)
    lse = jnp.where(some, m * SCALE2 + jnp.log2(total), LOW)
    return acc / total, lse


def merge_kernel(post_ref, ml_ref, acc_ref, got_ref, out_ref, ob_ref):
    for i in range(N):
        mine, lse_a = of_half(0, i, ml_ref, acc_ref)
        got = got_ref[i].astype(F32)
        lse_b = got[128:129] + got[129:130] + got[130:131]
        top = jnp.maximum(lse_a, lse_b)
        wa, wb = jnp.exp2(lse_a - top), jnp.exp2(lse_b - top)
        inv = 1.0 / (wa + wb)
        o = (mine * (wa * inv) + got[:128] * (wb * inv)).T.astype(BF)
        at = 0
        for row, rows, g in columns(i):
            ob_ref[row : row + rows, g * 128 : (g + 1) * 128] = o[at : at + rows]
            at += rows
    p = lax.broadcasted_iota(jnp.int32, (SHARDS * SLOTS, CAP), 1)
    spread = jnp.where(p == post_ref[...], 1.0, 0.0).astype(BF)
    out_ref[...] = jnp.dot(spread, ob_ref[...], preferred_element_type=F32).astype(BF)


def home_kernel(rot_ref, o_ref, out_ref):
    m = pack_matrix(rot_ref[0], True)
    for h in range(2):
        x = o_ref[:, h, :, :].reshape(ROWS, 512)
        out_ref[:, h * 512 : (h + 1) * 512] = jnp.dot(m, x, preferred_element_type=F32).astype(BF)


def own_kernel(hd_ref, own_ref, w_ref, out_ref):
    out_ref[...] = jnp.dot(own_ref[...], w_ref[...], preferred_element_type=F32)


def project_kernel(first_ref, other_ref, w_ref, gain_ref, live_ref, out_ref):
    s = first_ref[...] + jnp.dot(other_ref[...], w_ref[...], preferred_element_type=F32)
    s = s.astype(BF).astype(F32)
    out_ref[...] = jnp.where(live_ref[...] > 0, gain_ref[...] * s, 0.0).astype(BF)


def local(q_home, k_home, v_home, weight, router, positions, counts):
    d = lax.axis_index("ctx").astype(jnp.int32)
    hd = lax.axis_index("head").astype(jnp.int32)
    half_w = weight.shape[1] // 2

    to_send = lax.dynamic_slice_in_dim(weight, (1 - hd) * half_w, half_w, axis=1)
    w_other = lax.ppermute(to_send, "head", [(0, 1), (1, 0)])

    freqs = THETA ** (-(jnp.arange(64, dtype=F32) * 2.0 / HEAD_WIDTH))
    angles = positions.astype(F32)[:, None] * jnp.concatenate([freqs, freqs])[None, :]
    sign = jnp.where(jnp.arange(128) < 64, -1.0, 1.0).astype(F32)
    cos, sin = jnp.cos(angles), jnp.sin(angles) * sign[None, :]
    rot = (d % 64).reshape(1)

    packed = pl.pallas_call(
        pack_kernel,
        out_shape=jax.ShapeDtypeStruct((32, 2, 16, 768), BF),
        in_specs=[SMEM] + [VMEM] * 5,
        out_specs=VMEM,
        compiler_params=params(32),
        name="pack",
    )(rot, q_home, k_home, v_home, cos, sin)
    got = lax.all_to_all(packed.reshape(1024, 768), "ctx", 0, 0, tiled=True)
    all_counts = lax.all_gather(counts, "ctx", axis=0, tiled=True)

    z, x, yl = d // 16, d // 4 % 4, d % 2
    dz = jnp.asarray(np.array(ring_steps(8), np.int32))
    dx = jnp.asarray(np.array(ring_steps(4), np.int32))
    member = ((z + dz) % 8)[:, None] * 8 + ((x + dx) % 4)[None, :] * 2 + yl
    partner = z * 8 + x * 2 + (1 - yl)
    member = jnp.concatenate([member.reshape(32), partner.reshape(1)])
    shard = jnp.arange(SHARDS, dtype=jnp.int32)

    def layout(who, all_counts):
        offset = (who[:, None] - shard[None, :]) % 64
        held = jnp.maximum((all_counts[None, :] - offset + 63) // 64, 0)
        before = (shard[:, None] < shard[None, :]).astype(BF)
        start = jnp.dot(held.astype(BF), before, preferred_element_type=F32).astype(jnp.int32)
        return offset, held, start

    _, held, start = layout(member[:1], all_counts)
    slot = jnp.arange(SLOTS, dtype=jnp.int32)[None, :]
    pos = jnp.where(slot < held[0][:, None], start[0][:, None] + slot, -1).reshape(-1)
    _, loads, _ = layout(jnp.arange(64, dtype=jnp.int32), all_counts)
    most = jnp.max(jnp.sum(loads, axis=1))

    def attention(kv_cap, got, all_counts, pos):
        kv_own, q_own = pl.pallas_call(
            compact_kernel,
            out_shape=(
                jax.ShapeDtypeStruct((kv_cap, 256), BF),
                jax.ShapeDtypeStruct((N, 4 * T, 128), BF),
            ),
            in_specs=[VMEM] * 2,
            out_specs=(VMEM, VMEM),
            compiler_params=params(16),
            name="compact",
        )(pos[None, :], got)
        kv_own, q_own, counts_now = lax.optimization_barrier((kv_own, q_own, all_counts))
        q_partner = hop(q_own, "y")

        offset, held, start = layout(member, counts_now)
        base = (shard[None, :] * ROWS + offset - 64 * start).astype(F32)
        place = jnp.arange(CAP, dtype=jnp.int32)[None, None, :]
        inside = (start[:, :, None] <= place) & (place < (start + held)[:, :, None])
        ids = jnp.sum(jnp.where(inside, base[:, :, None] + (64 * place).astype(F32), 0.0), axis=1)
        ids = jnp.where(place[0] < jnp.sum(held, axis=1)[:, None], ids, BIG)
        q_rows = jnp.stack([ids[0], ids[32]])
        best = jnp.max(jnp.where(q_rows >= BIG, -1.0, q_rows), axis=0)
        edges = [i * T for i in range(N)] + [CAP - 32, CAP]
        q_max = jnp.stack([jnp.max(best[a:b]) for a, b in zip(edges, edges[1:])])
        live = (q_max >= 0.0).astype(jnp.int32)
        reach = jnp.sum((ids[:32, None, :] <= q_max[None, :, None]).astype(jnp.int32), axis=2)
        reach = jnp.max(reach.reshape(8, 4, TILES), axis=1)
        more = jnp.maximum(reach - jnp.asarray(REACH, jnp.int32)[None, :] + MORE - 1, 0) // MORE
        q_tiles = q_rows[:, : CAP - T].reshape(2, N - 1, 1, T)
        q_ids = jnp.tile(q_tiles[:, :, :, :], (1, 1, 4, 1)).reshape(2, N - 1, 1, 4 * T)
        q_last = jnp.tile(q_rows[:, CAP - T :].reshape(2, 2, 1, 32), (1, 1, 4, 1))
        q_ids = jnp.concatenate([q_ids, q_last.reshape(2, 1, 1, 4 * T)], axis=1)
        slab_ids = ids[:32, :kv_cap].reshape(8, 4, kv_cap, 1)

        slab = jnp.stack(ring(kv_own, "x", 4, 0))
        slab, q_partner = lax.optimization_barrier((slab, q_partner))
        slabs = ring(slab, "z", 8, 1)
        state = ()
        chunks = ((0,), (1, 2), (3, 4), (5, 6), (7,))
        for c, chunk in enumerate(chunks):
            first, last, n = c == 0, c == len(chunks) - 1, len(chunk)
            steps = jnp.max(more[chunk[0] : chunk[-1] + 1], axis=0)
            k_ids = jnp.broadcast_to(slab_ids[chunk[0] : chunk[-1] + 1], (n, 4, kv_cap, 128))
            shapes = [
                jax.ShapeDtypeStruct((2, N, 8, 4 * T), F32),
                jax.ShapeDtypeStruct((2, N, 128, 4 * T), F32),
            ]
            if last:
                shapes.append(jax.ShapeDtypeStruct((N, 128 + EXTRA, 4 * T), BF))
            state = pl.pallas_call(
                functools.partial(attend_kernel, n, first, last),
                out_shape=tuple(shapes),
                in_specs=[SMEM] * 2 + [VMEM] * (4 + n + len(state)),
                out_specs=(VMEM,) * len(shapes),
                input_output_aliases={} if first else {6 + n: 0, 7 + n: 1},
                compiler_params=params(48),
                cost_estimate=pl.CostEstimate(
                    flops=n * 4_000_000_000, bytes_accessed=n * 4_000_000, transcendentals=n * 2_000_000
                ),
                name="attend",
            )(steps, live, q_ids, k_ids, q_own, q_partner, *[slabs[k] for k in chunk], *state)
        ml, acc, message = state
        theirs = hop(message, "y")

        return pl.pallas_call(
            merge_kernel,
            out_shape=jax.ShapeDtypeStruct((1024, 512), BF),
            in_specs=[VMEM] * 4,
            out_specs=VMEM,
            scratch_shapes=[pltpu.VMEM((CAP, 512), BF)],
            compiler_params=params(24),
            name="merge",
        )(pos[:, None], ml, acc, theirs)

    o_packed = lax.cond(
        most <= USUAL,
        functools.partial(attention, USUAL),
        functools.partial(attention, CAP),
        got,
        all_counts,
        pos,
    )
    o_got = lax.all_to_all(o_packed, "ctx", 0, 0, tiled=True)
    o_home = pl.pallas_call(
        home_kernel,
        out_shape=jax.ShapeDtypeStruct((ROWS, 1024), BF),
        in_specs=[SMEM, VMEM],
        out_specs=VMEM,
        compiler_params=params(16),
        name="home",
    )(rot, o_got.reshape(32, 2, 16, 512))
    o_other = lax.ppermute(o_home, "head", [(0, 1), (1, 0)])

    live = (jnp.arange(ROWS, dtype=jnp.int32) < counts[0]).astype(jnp.int32)
    cols = 512
    steps = half_w // cols
    first = pl.pallas_call(
        own_kernel,
        out_shape=jax.ShapeDtypeStruct((ROWS, half_w), F32),
        grid_spec=pltpu.PrefetchScalarGridSpec(
            num_scalar_prefetch=1,
            grid=(steps,),
            in_specs=[
                pl.BlockSpec((ROWS, 1024), lambda i, h: (0, 0)),
                pl.BlockSpec((1024, cols), lambda i, h: (0, h[0] * steps + i)),
            ],
            out_specs=pl.BlockSpec((ROWS, cols), lambda i, h: (0, i)),
        ),
        compiler_params=params(56),
        cost_estimate=pl.CostEstimate(
            flops=2_200_000_000, bytes_accessed=9_000_000, transcendentals=0
        ),
        name="project_own",
    )(hd.reshape(1), o_home, weight)
    return pl.pallas_call(
        project_kernel,
        out_shape=jax.ShapeDtypeStruct((ROWS, half_w), BF),
        grid=(steps,),
        in_specs=[
            pl.BlockSpec((ROWS, cols), lambda i: (0, i)),
            pl.BlockSpec((ROWS, 1024), lambda i: (0, 0)),
            pl.BlockSpec((1024, cols), lambda i: (0, i)),
            pl.BlockSpec((ROWS, 1), lambda i: (0, 0)),
            pl.BlockSpec((ROWS, 1), lambda i: (0, 0)),
        ],
        out_specs=pl.BlockSpec((ROWS, cols), lambda i: (0, i)),
        compiler_params=params(56),
        name="project",
    )(first, o_other, w_other, router[:, None], live[:, None])


def solution(mesh):
    return jax.shard_map(
        local,
        mesh=mesh,
        in_specs=(
            P("ctx", "head"),
            P("ctx", "head"),
            P("ctx", "head"),
            P("head", None),
            P("ctx"),
            P("ctx"),
            P("ctx"),
        ),
        out_specs=P("ctx", "head"),
        check_vma=False,
    )
```

```python
import functools

import jax
import jax.numpy as jnp
import numpy as np
from jax import lax
from jax.experimental import pallas as pl
from jax.experimental.pallas import tpu as pltpu
from jax.sharding import PartitionSpec as P

HEAD_WIDTH = 128
THETA = 500000.0
CAP = 320
SLOTS = 8
SHARDS = 128
ROWS = 512
T = 64
N = CAP // T
TILES = N + 1
REACH = (80, 144, 208, 272, 272, 272)
MORE = 16
BIG = float(1 << 30)
LOW = -1e30
EXTRA = 16
BF = jnp.bfloat16
F32 = jnp.float32
SCALE2 = float(1.0 / np.sqrt(128.0) * np.log2(np.e))
VMEM = pl.BlockSpec(memory_space=pltpu.VMEM)
SMEM = pl.BlockSpec(memory_space=pltpu.SMEM)


def params(mib):
    return pltpu.CompilerParams(vmem_limit_bytes=mib * 2**20)


def perm_of(axis, k):
    pairs = []
    for d in range(SHARDS):
        z, x, y = d // 16, d // 4 % 4, d % 4
        if axis == "z":
            z = (z + k) % 8
        elif axis == "x":
            x = (x + k) % 4
        else:
            y = y ^ 1
        pairs.append((d, z * 16 + x * 4 + y))
    return pairs


def hop(a, axis, k=1):
    return lax.ppermute(a, "ctx", perm_of(axis, k))


def ring(a, axis, size, row_dim):
    half = a.shape[row_dim] // 2
    out, up, down = [a], a, a
    for _ in range(size // 2 - 1):
        up, down = hop(up, axis, 1), hop(down, axis, -1)
        out += [up, down]
    lo = hop(lax.slice_in_dim(up, 0, half, axis=row_dim), axis, 1)
    hi = hop(lax.slice_in_dim(down, half, 2 * half, axis=row_dim), axis, -1)
    out.append(jnp.concatenate([lo, hi], axis=row_dim))
    return out


def ring_steps(size):
    steps = [0]
    for i in range(1, size // 2):
        steps += [-i, i]
    return steps + [size // 2]


def pack_matrix(rot, transpose):
    packed_dim = 1 if transpose else 0
    o = lax.broadcasted_iota(jnp.int32, (ROWS, ROWS), packed_dim)
    s = lax.broadcasted_iota(jnp.int32, (ROWS, ROWS), 1 - packed_dim)
    src = (o & 7) * 64 + (((o >> 3) + 64 - rot) & 63)
    return jnp.where(src == s, 1.0, 0.0).astype(BF)


def pack_kernel(rot_ref, q_ref, k_ref, v_ref, cos_ref, sin_ref, out_ref):
    cos, sin = cos_ref[...], sin_ref[...]

    def rotate(x):
        x = x.astype(F32)
        return (x * cos + pltpu.roll(x, 64, 1) * sin).astype(BF)

    m = pack_matrix(rot_ref[0], False)
    for h in range(2):
        parts = [rotate(q_ref[:, h * 512 + g * 128 : h * 512 + (g + 1) * 128]) for g in range(4)]
        parts.append(rotate(k_ref[:, h * 128 : (h + 1) * 128]))
        parts.append(v_ref[:, h * 128 : (h + 1) * 128])
        for c, x in enumerate(parts):
            y = jnp.dot(m, x, preferred_element_type=F32).astype(BF)
            out_ref[:, h, :, c * 128 : (c + 1) * 128] = y.reshape(32, 16, 128)


def compact_matrix(pos):
    p = lax.broadcasted_iota(jnp.int32, (CAP, SHARDS * SLOTS), 0)
    return jnp.where(p == pos, 1.0, 0.0).astype(BF)


def columns(i):
    if i < N - 1:
        return [(i * T, T, g) for g in range(4)]
    return [(i * T + b * 32, 32, g) for b in range(2) for g in range(4)]


def compact_kernel(pos_ref, x_ref, kv_ref, q_ref):
    m = compact_matrix(pos_ref[...])
    kv_ref[...] = jnp.dot(m, x_ref[:, 512:], preferred_element_type=F32).astype(BF)
    y = jnp.dot(m, x_ref[:, :512], preferred_element_type=F32).astype(BF)
    for i in range(N):
        at = 0
        for row, rows, g in columns(i):
            q_ref[i, at : at + rows, :] = y[row : row + rows, g * 128 : (g + 1) * 128]
            at += rows


def attend_kernel(n, first, last, *refs):
    more_ref, live_ref, qid_ref, kid_ref, qa_ref, qb_ref = refs[:6]
    kv_refs, refs = refs[6 : 6 + n], refs[6 + n :]
    if not first:
        refs = refs[2:]
    ml_ref, acc_ref = refs[:2]
    if first:
        row = lax.broadcasted_iota(jnp.int32, ml_ref.shape, 2)
        ml_ref[...] = jnp.where(row == 0, LOW, 0.0)
        acc_ref[...] = jnp.zeros_like(acc_ref)

    def batch(tiles, start, rows):
        at = pl.ds(start, rows)
        keys = [kv[:, at, :128].reshape(4 * rows, 128) for kv in kv_refs]
        vals = [kv[:, at, 128:].reshape(4 * rows, 128) for kv in kv_refs]
        kids = []
        for c in range(n):
            col = kid_ref[c, :, at, :].reshape(4 * rows, 128)
            kids.append(jnp.concatenate([col, col], axis=1))
        old = [(ml_ref[h, i, 0:1, :], ml_ref[h, i, 1:2, :], acc_ref[h, i]) for _, _, h, i in tiles]
        found = []
        for (q, qid, _, _), (m, _, _) in zip(tiles, old):
            scores = []
            for key, kid in zip(keys, kids):
                s = lax.dot_general(key, q, (((1,), (1,)), ((), ())), preferred_element_type=F32)
                s = jnp.where(kid <= qid, s, LOW)
                m = jnp.maximum(m, jnp.max(s, axis=0, keepdims=True))
                scores.append(s)
            found.append((scores, m))
        done = []
        for (scores, new), (m, total, acc) in zip(found, old):
            keep = jnp.exp2((m - new) * SCALE2)
            total, acc = total * keep, acc * keep
            for s, val in zip(scores, vals):
                p = jnp.exp2((s - new) * SCALE2)
                total = total + jnp.sum(p, axis=0, keepdims=True)
                acc = acc + lax.dot_general(
                    val, p.astype(BF), (((0,), (0,)), ((), ())), preferred_element_type=F32
                )
            done.append((new, total, acc))
        for (_, _, h, i), (m, total, acc) in zip(tiles, done):
            ml_ref[h, i, 0:1, :] = m
            ml_ref[h, i, 1:2, :] = total
            acc_ref[h, i] = acc

    def visit(i):
        if i < N - 1:
            tiles = [(qa_ref[i], qid_ref[0, i], 0, i), (qb_ref[i], qid_ref[1, i], 1, i)]
        else:
            b = i - (N - 1)
            c = slice(b * 128, (b + 1) * 128)
            q = jnp.concatenate([qa_ref[N - 1, c], qb_ref[N - 1, c]], axis=0)
            qid = jnp.concatenate([qid_ref[0, N - 1, :, c], qid_ref[1, N - 1, :, c]], axis=1)
            tiles = [(q, qid, b, N - 1)]
        batch(tiles, 0, REACH[i])

        def further(e, _):
            batch(tiles, pl.multiple_of(REACH[i] + e * MORE, MORE), MORE)
            return 0

        lax.fori_loop(0, more_ref[i], further, 0)

    for i in range(TILES):
        if i < N - 1:
            visit(i)
        else:
            pl.when(live_ref[i] > 0)(functools.partial(visit, i))
    if last:
        for i in range(N):
            o, lse = of_half(1, i, ml_ref, acc_ref)
            hi = lse.astype(BF).astype(F32)
            mid = (lse - hi).astype(BF).astype(F32)
            lo = lse - hi - mid
            row = lax.broadcasted_iota(jnp.int32, (EXTRA, 4 * T), 0)
            note = jnp.where(row == 0, hi, jnp.where(row == 1, mid, jnp.where(row == 2, lo, 0.0)))
            refs[2][i, :128, :] = o.astype(BF)
            refs[2][i, 128:, :] = note.astype(BF)


def of_half(half, i, ml_ref, acc_ref):
    if i < N - 1:
        return finish(ml_ref[half, i], acc_ref[half, i])
    c = slice(half * 128, (half + 1) * 128)
    ml = jnp.concatenate([ml_ref[0, i, :, c], ml_ref[1, i, :, c]], axis=1)
    acc = jnp.concatenate([acc_ref[0, i, :, c], acc_ref[1, i, :, c]], axis=1)
    return finish(ml, acc)


def finish(ml, acc):
    m, total = ml[0:1], ml[1:2]
    some = total > 0.0
    total = jnp.where(some, total, 1.0)
    lse = jnp.where(some, m * SCALE2 + jnp.log2(total), LOW)
    return acc / total, lse


def merge_kernel(post_ref, ml_ref, acc_ref, got_ref, out_ref, ob_ref):
    for i in range(N):
        mine, lse_a = of_half(0, i, ml_ref, acc_ref)
        got = got_ref[i].astype(F32)
        lse_b = got[128:129] + got[129:130] + got[130:131]
        top = jnp.maximum(lse_a, lse_b)
        wa, wb = jnp.exp2(lse_a - top), jnp.exp2(lse_b - top)
        inv = 1.0 / (wa + wb)
        o = (mine * (wa * inv) + got[:128] * (wb * inv)).T.astype(BF)
        at = 0
        for row, rows, g in columns(i):
            ob_ref[row : row + rows, g * 128 : (g + 1) * 128] = o[at : at + rows]
            at += rows
    p = lax.broadcasted_iota(jnp.int32, (SHARDS * SLOTS, CAP), 1)
    spread = jnp.where(p == post_ref[...], 1.0, 0.0).astype(BF)
    out_ref[...] = jnp.dot(spread, ob_ref[...], preferred_element_type=F32).astype(BF)


def home_kernel(rot_ref, o_ref, out_ref):
    m = pack_matrix(rot_ref[0], True)
    for h in range(2):
        x = o_ref[:, h, :, :].reshape(ROWS, 512)
        out_ref[:, h * 512 : (h + 1) * 512] = jnp.dot(m, x, preferred_element_type=F32).astype(BF)


def project_kernel(hd_ref, own_ref, other_ref, wa_ref, wb_ref, gain_ref, live_ref, out_ref):
    s = jnp.dot(own_ref[...], wa_ref[...], preferred_element_type=F32)
    s = s + jnp.dot(other_ref[...], wb_ref[...], preferred_element_type=F32)
    s = s.astype(BF).astype(F32)
    out_ref[...] = jnp.where(live_ref[...] > 0, gain_ref[...] * s, 0.0).astype(BF)


def local(q_home, k_home, v_home, weight, router, positions, counts):
    d = lax.axis_index("ctx").astype(jnp.int32)
    hd = lax.axis_index("head").astype(jnp.int32)
    half_w = weight.shape[1] // 2

    to_send = lax.dynamic_slice_in_dim(weight, (1 - hd) * half_w, half_w, axis=1)
    w_other = lax.ppermute(to_send, "head", [(0, 1), (1, 0)])

    freqs = THETA ** (-(jnp.arange(64, dtype=F32) * 2.0 / HEAD_WIDTH))
    angles = positions.astype(F32)[:, None] * jnp.concatenate([freqs, freqs])[None, :]
    sign = jnp.where(jnp.arange(128) < 64, -1.0, 1.0).astype(F32)
    cos, sin = jnp.cos(angles), jnp.sin(angles) * sign[None, :]
    rot = (d % 64).reshape(1)

    packed = pl.pallas_call(
        pack_kernel,
        out_shape=jax.ShapeDtypeStruct((32, 2, 16, 768), BF),
        in_specs=[SMEM] + [VMEM] * 5,
        out_specs=VMEM,
        compiler_params=params(32),
        name="pack",
    )(rot, q_home, k_home, v_home, cos, sin)
    got = lax.all_to_all(packed.reshape(1024, 768), "ctx", 0, 0, tiled=True)
    all_counts = lax.all_gather(counts, "ctx", axis=0, tiled=True)

    z, x, yl = d // 16, d // 4 % 4, d % 2
    dz = jnp.asarray(np.array(ring_steps(8), np.int32))
    dx = jnp.asarray(np.array(ring_steps(4), np.int32))
    member = ((z + dz) % 8)[:, None] * 8 + ((x + dx) % 4)[None, :] * 2 + yl
    partner = z * 8 + x * 2 + (1 - yl)
    member = jnp.concatenate([member.reshape(32), partner.reshape(1)])
    shard = jnp.arange(SHARDS, dtype=jnp.int32)

    def layout(who, all_counts):
        offset = (who[:, None] - shard[None, :]) % 64
        held = jnp.maximum((all_counts[None, :] - offset + 63) // 64, 0)
        before = (shard[:, None] < shard[None, :]).astype(BF)
        start = jnp.dot(held.astype(BF), before, preferred_element_type=F32).astype(jnp.int32)
        return offset, held, start

    _, held, start = layout(member[:1], all_counts)
    slot = jnp.arange(SLOTS, dtype=jnp.int32)[None, :]
    pos = jnp.where(slot < held[0][:, None], start[0][:, None] + slot, -1).reshape(-1)
    kv_own, q_own = pl.pallas_call(
        compact_kernel,
        out_shape=(
            jax.ShapeDtypeStruct((CAP, 256), BF),
            jax.ShapeDtypeStruct((N, 4 * T, 128), BF),
        ),
        in_specs=[VMEM] * 2,
        out_specs=(VMEM, VMEM),
        compiler_params=params(16),
        name="compact",
    )(pos[None, :], got)
    kv_own, q_own, counts_now = lax.optimization_barrier((kv_own, q_own, all_counts))
    q_partner = hop(q_own, "y")

    offset, held, start = layout(member, counts_now)
    base = (shard[None, :] * ROWS + offset - 64 * start).astype(F32)
    place = jnp.arange(CAP, dtype=jnp.int32)[None, None, :]
    inside = (start[:, :, None] <= place) & (place < (start + held)[:, :, None])
    ids = jnp.sum(jnp.where(inside, base[:, :, None] + (64 * place).astype(F32), 0.0), axis=1)
    ids = jnp.where(place[0] < jnp.sum(held, axis=1)[:, None], ids, BIG)
    q_rows = jnp.stack([ids[0], ids[32]])
    best = jnp.max(jnp.where(q_rows >= BIG, -1.0, q_rows), axis=0)
    edges = [i * T for i in range(N)] + [CAP - 32, CAP]
    q_max = jnp.stack([jnp.max(best[a:b]) for a, b in zip(edges, edges[1:])])
    live = (q_max >= 0.0).astype(jnp.int32)
    reach = jnp.sum((ids[:32, None, :] <= q_max[None, :, None]).astype(jnp.int32), axis=2)
    reach = jnp.max(reach.reshape(8, 4, TILES), axis=1)
    more = jnp.maximum(reach - jnp.asarray(REACH, jnp.int32)[None, :] + MORE - 1, 0) // MORE
    q_tiles = q_rows[:, : CAP - T].reshape(2, N - 1, 1, T)
    q_ids = jnp.tile(q_tiles[:, :, :, :], (1, 1, 4, 1)).reshape(2, N - 1, 1, 4 * T)
    q_last = jnp.tile(q_rows[:, CAP - T :].reshape(2, 2, 1, 32), (1, 1, 4, 1))
    q_ids = jnp.concatenate([q_ids, q_last.reshape(2, 1, 1, 4 * T)], axis=1)
    slab_ids = ids[:32].reshape(8, 4, CAP, 1)

    slab = jnp.stack(ring(kv_own, "x", 4, 0))
    slab, q_partner = lax.optimization_barrier((slab, q_partner))
    slabs = ring(slab, "z", 8, 1)
    state = ()
    chunks = ((0,), (1, 2), (3, 4), (5, 6), (7,))
    for c, chunk in enumerate(chunks):
        first, last, n = c == 0, c == len(chunks) - 1, len(chunk)
        steps = jnp.max(more[chunk[0] : chunk[-1] + 1], axis=0)
        k_ids = jnp.broadcast_to(slab_ids[chunk[0] : chunk[-1] + 1], (n, 4, CAP, 128))
        shapes = [
            jax.ShapeDtypeStruct((2, N, 8, 4 * T), F32),
            jax.ShapeDtypeStruct((2, N, 128, 4 * T), F32),
        ]
        if last:
            shapes.append(jax.ShapeDtypeStruct((N, 128 + EXTRA, 4 * T), BF))
        state = pl.pallas_call(
            functools.partial(attend_kernel, n, first, last),
            out_shape=tuple(shapes),
            in_specs=[SMEM] * 2 + [VMEM] * (4 + n + len(state)),
            out_specs=(VMEM,) * len(shapes),
            input_output_aliases={} if first else {6 + n: 0, 7 + n: 1},
            compiler_params=params(48),
            cost_estimate=pl.CostEstimate(
                flops=n * 4_000_000_000, bytes_accessed=n * 4_000_000, transcendentals=n * 2_000_000
            ),
            name="attend",
        )(steps, live, q_ids, k_ids, q_own, q_partner, *[slabs[k] for k in chunk], *state)
    ml, acc, message = state
    theirs = hop(message, "y")

    o_packed = pl.pallas_call(
        merge_kernel,
        out_shape=jax.ShapeDtypeStruct((1024, 512), BF),
        in_specs=[VMEM] * 4,
        out_specs=VMEM,
        scratch_shapes=[pltpu.VMEM((CAP, 512), BF)],
        compiler_params=params(24),
        name="merge",
    )(pos[:, None], ml, acc, theirs)

    o_got = lax.all_to_all(o_packed, "ctx", 0, 0, tiled=True)
    o_home = pl.pallas_call(
        home_kernel,
        out_shape=jax.ShapeDtypeStruct((ROWS, 1024), BF),
        in_specs=[SMEM, VMEM],
        out_specs=VMEM,
        compiler_params=params(16),
        name="home",
    )(rot, o_got.reshape(32, 2, 16, 512))
    o_other = lax.ppermute(o_home, "head", [(0, 1), (1, 0)])

    live = (jnp.arange(ROWS, dtype=jnp.int32) < counts[0]).astype(jnp.int32)
    cols = 512
    steps = half_w // cols
    return pl.pallas_call(
        project_kernel,
        out_shape=jax.ShapeDtypeStruct((ROWS, half_w), BF),
        grid_spec=pltpu.PrefetchScalarGridSpec(
            num_scalar_prefetch=1,
            grid=(steps,),
            in_specs=[
                pl.BlockSpec((ROWS, 1024), lambda i, h: (0, 0)),
                pl.BlockSpec((ROWS, 1024), lambda i, h: (0, 0)),
                pl.BlockSpec((1024, cols), lambda i, h: (0, h[0] * steps + i)),
                pl.BlockSpec((1024, cols), lambda i, h: (0, i)),
                pl.BlockSpec((ROWS, 1), lambda i, h: (0, 0)),
                pl.BlockSpec((ROWS, 1), lambda i, h: (0, 0)),
            ],
            out_specs=pl.BlockSpec((ROWS, cols), lambda i, h: (0, i)),
        ),
        compiler_params=params(56),
        name="project",
    )(hd.reshape(1), o_home, o_other, weight, w_other, router[:, None], live[:, None])


def solution(mesh):
    return jax.shard_map(
        local,
        mesh=mesh,
        in_specs=(
            P("ctx", "head"),
            P("ctx", "head"),
            P("ctx", "head"),
            P("head", None),
            P("ctx"),
            P("ctx"),
            P("ctx"),
        ),
        out_specs=P("ctx", "head"),
        check_vma=False,
    )
```

```python
import functools

import jax
import jax.numpy as jnp
import numpy as np
from jax import lax
from jax.experimental import pallas as pl
from jax.experimental.pallas import tpu as pltpu
from jax.sharding import PartitionSpec as P

HEAD_WIDTH = 128
THETA = 500000.0
CAP = 320
SLOTS = 8
SHARDS = 128
ROWS = 512
T = 64
N = CAP // T
TILES = N + 1
REACH = (80, 144, 208, 272, 272, 272)
MORE = 16
BIG = float(1 << 30)
LOW = -1e30
EXTRA = 16
BF = jnp.bfloat16
F32 = jnp.float32
SCALE2 = float(1.0 / np.sqrt(128.0) * np.log2(np.e))
VMEM = pl.BlockSpec(memory_space=pltpu.VMEM)
SMEM = pl.BlockSpec(memory_space=pltpu.SMEM)


def params(mib):
    return pltpu.CompilerParams(vmem_limit_bytes=mib * 2**20)


def perm_of(axis, k):
    pairs = []
    for d in range(SHARDS):
        z, x, y = d // 16, d // 4 % 4, d % 4
        if axis == "z":
            z = (z + k) % 8
        elif axis == "x":
            x = (x + k) % 4
        else:
            y = y ^ 1
        pairs.append((d, z * 16 + x * 4 + y))
    return pairs


def hop(a, axis, k=1):
    return lax.ppermute(a, "ctx", perm_of(axis, k))


def ring(a, axis, size, row_dim):
    half = a.shape[row_dim] // 2
    out, up, down = [a], a, a
    for _ in range(size // 2 - 1):
        up, down = hop(up, axis, 1), hop(down, axis, -1)
        out += [up, down]
    lo = hop(lax.slice_in_dim(up, 0, half, axis=row_dim), axis, 1)
    hi = hop(lax.slice_in_dim(down, half, 2 * half, axis=row_dim), axis, -1)
    out.append(jnp.concatenate([lo, hi], axis=row_dim))
    return out


def ring_steps(size):
    steps = [0]
    for i in range(1, size // 2):
        steps += [-i, i]
    return steps + [size // 2]


def pack_matrix(rot, transpose):
    packed_dim = 1 if transpose else 0
    o = lax.broadcasted_iota(jnp.int32, (ROWS, ROWS), packed_dim)
    s = lax.broadcasted_iota(jnp.int32, (ROWS, ROWS), 1 - packed_dim)
    src = (o & 7) * 64 + (((o >> 3) + 64 - rot) & 63)
    return jnp.where(src == s, 1.0, 0.0).astype(BF)


def pack_kernel(rot_ref, q_ref, k_ref, v_ref, cos_ref, sin_ref, out_ref):
    cos, sin = cos_ref[...], sin_ref[...]

    def rotate(x):
        x = x.astype(F32)
        return (x * cos + pltpu.roll(x, 64, 1) * sin).astype(BF)

    m = pack_matrix(rot_ref[0], False)
    for h in range(2):
        parts = [rotate(q_ref[:, h * 512 + g * 128 : h * 512 + (g + 1) * 128]) for g in range(4)]
        parts.append(rotate(k_ref[:, h * 128 : (h + 1) * 128]))
        parts.append(v_ref[:, h * 128 : (h + 1) * 128])
        for c, x in enumerate(parts):
            y = jnp.dot(m, x, preferred_element_type=F32).astype(BF)
            out_ref[:, h, :, c * 128 : (c + 1) * 128] = y.reshape(32, 16, 128)


def compact_matrix(pos):
    p = lax.broadcasted_iota(jnp.int32, (CAP, SHARDS * SLOTS), 0)
    return jnp.where(p == pos, 1.0, 0.0).astype(BF)


def columns(i):
    if i < N - 1:
        return [(i * T, T, g) for g in range(4)]
    return [(i * T + b * 32, 32, g) for b in range(2) for g in range(4)]


def compact_kernel(pos_ref, x_ref, kv_ref, q_ref):
    m = compact_matrix(pos_ref[...])
    kv_ref[...] = jnp.dot(m, x_ref[:, 512:], preferred_element_type=F32).astype(BF)
    y = jnp.dot(m, x_ref[:, :512], preferred_element_type=F32).astype(BF)
    for i in range(N):
        at = 0
        for row, rows, g in columns(i):
            q_ref[i, at : at + rows, :] = y[row : row + rows, g * 128 : (g + 1) * 128]
            at += rows


def attend_kernel(n, first, last, *refs):
    more_ref, live_ref, qid_ref, kid_ref, qa_ref, qb_ref = refs[:6]
    kv_refs, refs = refs[6 : 6 + n], refs[6 + n :]
    if not first:
        refs = refs[2:]
    ml_ref, acc_ref = refs[:2]
    if first:
        row = lax.broadcasted_iota(jnp.int32, ml_ref.shape, 2)
        ml_ref[...] = jnp.where(row == 0, LOW, 0.0)
        acc_ref[...] = jnp.zeros_like(acc_ref)

    def batch(tiles, start, rows):
        at = pl.ds(start, rows)
        keys = [kv[:, at, :128].reshape(4 * rows, 128) for kv in kv_refs]
        vals = [kv[:, at, 128:].reshape(4 * rows, 128) for kv in kv_refs]
        kids = []
        for c in range(n):
            col = kid_ref[c, :, at, :].reshape(4 * rows, 128)
            kids.append(jnp.concatenate([col, col], axis=1))
        old = [(ml_ref[h, i, 0:1, :], ml_ref[h, i, 1:2, :], acc_ref[h, i]) for _, _, h, i in tiles]
        found = []
        for (q, qid, _, _), (m, _, _) in zip(tiles, old):
            scores = []
            for key, kid in zip(keys, kids):
                s = lax.dot_general(key, q, (((1,), (1,)), ((), ())), preferred_element_type=F32)
                s = jnp.where(kid <= qid, s, LOW)
                m = jnp.maximum(m, jnp.max(s, axis=0, keepdims=True))
                scores.append(s)
            found.append((scores, m))
        done = []
        for (scores, new), (m, total, acc) in zip(found, old):
            keep = jnp.exp2((m - new) * SCALE2)
            total, acc = total * keep, acc * keep
            for s, val in zip(scores, vals):
                p = jnp.exp2((s - new) * SCALE2)
                total = total + jnp.sum(p, axis=0, keepdims=True)
                acc = acc + lax.dot_general(
                    val, p.astype(BF), (((0,), (0,)), ((), ())), preferred_element_type=F32
                )
            done.append((new, total, acc))
        for (_, _, h, i), (m, total, acc) in zip(tiles, done):
            ml_ref[h, i, 0:1, :] = m
            ml_ref[h, i, 1:2, :] = total
            acc_ref[h, i] = acc

    def visit(i):
        if i < N - 1:
            tiles = [(qa_ref[i], qid_ref[0, i], 0, i), (qb_ref[i], qid_ref[1, i], 1, i)]
        else:
            b = i - (N - 1)
            c = slice(b * 128, (b + 1) * 128)
            q = jnp.concatenate([qa_ref[N - 1, c], qb_ref[N - 1, c]], axis=0)
            qid = jnp.concatenate([qid_ref[0, N - 1, :, c], qid_ref[1, N - 1, :, c]], axis=1)
            tiles = [(q, qid, b, N - 1)]
        batch(tiles, 0, REACH[i])

        def further(e, _):
            batch(tiles, pl.multiple_of(REACH[i] + e * MORE, MORE), MORE)
            return 0

        lax.fori_loop(0, more_ref[i], further, 0)

    for i in range(TILES):
        if i < N - 1:
            visit(i)
        else:
            pl.when(live_ref[i] > 0)(functools.partial(visit, i))
    if last:
        for i in range(N):
            o, lse = of_half(1, i, ml_ref, acc_ref)
            hi = lse.astype(BF).astype(F32)
            mid = (lse - hi).astype(BF).astype(F32)
            lo = lse - hi - mid
            row = lax.broadcasted_iota(jnp.int32, (EXTRA, 4 * T), 0)
            note = jnp.where(row == 0, hi, jnp.where(row == 1, mid, jnp.where(row == 2, lo, 0.0)))
            refs[2][i, :128, :] = o.astype(BF)
            refs[2][i, 128:, :] = note.astype(BF)


def of_half(half, i, ml_ref, acc_ref):
    if i < N - 1:
        return finish(ml_ref[half, i], acc_ref[half, i])
    c = slice(half * 128, (half + 1) * 128)
    ml = jnp.concatenate([ml_ref[0, i, :, c], ml_ref[1, i, :, c]], axis=1)
    acc = jnp.concatenate([acc_ref[0, i, :, c], acc_ref[1, i, :, c]], axis=1)
    return finish(ml, acc)


def finish(ml, acc):
    m, total = ml[0:1], ml[1:2]
    some = total > 0.0
    total = jnp.where(some, total, 1.0)
    lse = jnp.where(some, m * SCALE2 + jnp.log2(total), LOW)
    return acc / total, lse


def merge_kernel(post_ref, ml_ref, acc_ref, got_ref, out_ref, ob_ref):
    for i in range(N):
        mine, lse_a = of_half(0, i, ml_ref, acc_ref)
        got = got_ref[i].astype(F32)
        lse_b = got[128:129] + got[129:130] + got[130:131]
        top = jnp.maximum(lse_a, lse_b)
        wa, wb = jnp.exp2(lse_a - top), jnp.exp2(lse_b - top)
        inv = 1.0 / (wa + wb)
        o = (mine * (wa * inv) + got[:128] * (wb * inv)).T.astype(BF)
        at = 0
        for row, rows, g in columns(i):
            ob_ref[row : row + rows, g * 128 : (g + 1) * 128] = o[at : at + rows]
            at += rows
    p = lax.broadcasted_iota(jnp.int32, (SHARDS * SLOTS, CAP), 1)
    spread = jnp.where(p == post_ref[...], 1.0, 0.0).astype(BF)
    out_ref[...] = jnp.dot(spread, ob_ref[...], preferred_element_type=F32).astype(BF)


def home_kernel(rot_ref, o_ref, out_ref):
    m = pack_matrix(rot_ref[0], True)
    for h in range(2):
        x = o_ref[:, h, :, :].reshape(ROWS, 512)
        out_ref[:, h * 512 : (h + 1) * 512] = jnp.dot(m, x, preferred_element_type=F32).astype(BF)


def project_kernel(hd_ref, own_ref, other_ref, wa_ref, wb_ref, gain_ref, out_ref):
    s = jnp.dot(own_ref[...], wa_ref[...], preferred_element_type=F32)
    s = s + jnp.dot(other_ref[...], wb_ref[...], preferred_element_type=F32)
    s = s.astype(BF).astype(F32)
    gain = gain_ref[...]
    out_ref[...] = jnp.where(gain != 0.0, gain * s, 0.0).astype(BF)


def local(q_home, k_home, v_home, weight, router, positions, counts):
    d = lax.axis_index("ctx").astype(jnp.int32)
    hd = lax.axis_index("head").astype(jnp.int32)
    half_w = weight.shape[1] // 2

    to_send = lax.dynamic_slice_in_dim(weight, (1 - hd) * half_w, half_w, axis=1)
    w_other = lax.ppermute(to_send, "head", [(0, 1), (1, 0)])

    freqs = THETA ** (-(jnp.arange(64, dtype=F32) * 2.0 / HEAD_WIDTH))
    angles = positions.astype(F32)[:, None] * jnp.concatenate([freqs, freqs])[None, :]
    sign = jnp.where(jnp.arange(128) < 64, -1.0, 1.0).astype(F32)
    cos, sin = jnp.cos(angles), jnp.sin(angles) * sign[None, :]
    rot = (d % 64).reshape(1)

    packed = pl.pallas_call(
        pack_kernel,
        out_shape=jax.ShapeDtypeStruct((32, 2, 16, 768), BF),
        in_specs=[SMEM] + [VMEM] * 5,
        out_specs=VMEM,
        compiler_params=params(32),
        name="pack",
    )(rot, q_home, k_home, v_home, cos, sin)
    got = lax.all_to_all(packed.reshape(1024, 768), "ctx", 0, 0, tiled=True)
    all_counts = lax.all_gather(counts, "ctx", axis=0, tiled=True)

    z, x, yl = d // 16, d // 4 % 4, d % 2
    dz = jnp.asarray(np.array(ring_steps(8), np.int32))
    dx = jnp.asarray(np.array(ring_steps(4), np.int32))
    member = ((z + dz) % 8)[:, None] * 8 + ((x + dx) % 4)[None, :] * 2 + yl
    partner = z * 8 + x * 2 + (1 - yl)
    member = jnp.concatenate([member.reshape(32), partner.reshape(1)])
    shard = jnp.arange(SHARDS, dtype=jnp.int32)

    def layout(who, all_counts):
        offset = (who[:, None] - shard[None, :]) % 64
        held = jnp.maximum((all_counts[None, :] - offset + 63) // 64, 0)
        before = (shard[:, None] < shard[None, :]).astype(BF)
        start = jnp.dot(held.astype(BF), before, preferred_element_type=F32).astype(jnp.int32)
        return offset, held, start

    _, held, start = layout(member[:1], all_counts)
    slot = jnp.arange(SLOTS, dtype=jnp.int32)[None, :]
    pos = jnp.where(slot < held[0][:, None], start[0][:, None] + slot, -1).reshape(-1)
    kv_own, q_own = pl.pallas_call(
        compact_kernel,
        out_shape=(
            jax.ShapeDtypeStruct((CAP, 256), BF),
            jax.ShapeDtypeStruct((N, 4 * T, 128), BF),
        ),
        in_specs=[VMEM] * 2,
        out_specs=(VMEM, VMEM),
        compiler_params=params(16),
        name="compact",
    )(pos[None, :], got)
    kv_own, q_own, counts_now = lax.optimization_barrier((kv_own, q_own, all_counts))
    q_partner = hop(q_own, "y")
    slab = jnp.stack(ring(kv_own, "x", 4, 0))
    own_live = jnp.arange(ROWS, dtype=jnp.int32) < counts[0]
    gain = jnp.where(own_live, router, 0.0)[:, None]
    slab, q_partner, gain = lax.optimization_barrier((slab, q_partner, gain))
    slabs = ring(slab, "z", 8, 1)

    offset, held, start = layout(member, counts_now)
    base = (shard[None, :] * ROWS + offset - 64 * start).astype(F32)
    place = jnp.arange(CAP, dtype=jnp.int32)[None, None, :]
    inside = (start[:, :, None] <= place) & (place < (start + held)[:, :, None])
    ids = jnp.sum(jnp.where(inside, base[:, :, None] + (64 * place).astype(F32), 0.0), axis=1)
    ids = jnp.where(place[0] < jnp.sum(held, axis=1)[:, None], ids, BIG)
    q_rows = jnp.stack([ids[0], ids[32]])
    best = jnp.max(jnp.where(q_rows >= BIG, -1.0, q_rows), axis=0)
    tile_of = np.minimum(np.arange(CAP) // T, N - 1) + (np.arange(CAP) >= CAP - 32)
    here = jnp.asarray(tile_of[None, :] == np.arange(TILES)[:, None])
    q_max = jnp.max(jnp.where(here, best[None, :], -1.0), axis=1)
    live = (q_max >= 0.0).astype(jnp.int32)
    reach = jnp.sum((ids[:32, None, :] <= q_max[None, :, None]).astype(jnp.int32), axis=2)
    reach = jnp.max(reach.reshape(8, 4, TILES), axis=1)
    more = jnp.maximum(reach - jnp.asarray(REACH, jnp.int32)[None, :] + MORE - 1, 0) // MORE
    q_tiles = q_rows[:, : CAP - T].reshape(2, N - 1, 1, T)
    q_ids = jnp.tile(q_tiles[:, :, :, :], (1, 1, 4, 1)).reshape(2, N - 1, 1, 4 * T)
    q_last = jnp.tile(q_rows[:, CAP - T :].reshape(2, 2, 1, 32), (1, 1, 4, 1))
    q_ids = jnp.concatenate([q_ids, q_last.reshape(2, 1, 1, 4 * T)], axis=1)
    slab_ids = ids[:32].reshape(8, 4, CAP, 1)

    state = ()
    chunks = ((0,), (1, 2), (3, 4), (5, 6), (7,))
    for c, chunk in enumerate(chunks):
        first, last, n = c == 0, c == len(chunks) - 1, len(chunk)
        steps = jnp.max(more[chunk[0] : chunk[-1] + 1], axis=0)
        k_ids = jnp.broadcast_to(slab_ids[chunk[0] : chunk[-1] + 1], (n, 4, CAP, 128))
        shapes = [
            jax.ShapeDtypeStruct((2, N, 8, 4 * T), F32),
            jax.ShapeDtypeStruct((2, N, 128, 4 * T), F32),
        ]
        if last:
            shapes.append(jax.ShapeDtypeStruct((N, 128 + EXTRA, 4 * T), BF))
        state = pl.pallas_call(
            functools.partial(attend_kernel, n, first, last),
            out_shape=tuple(shapes),
            in_specs=[SMEM] * 2 + [VMEM] * (4 + n + len(state)),
            out_specs=(VMEM,) * len(shapes),
            input_output_aliases={} if first else {6 + n: 0, 7 + n: 1},
            compiler_params=params(48),
            cost_estimate=pl.CostEstimate(
                flops=n * 4_000_000_000, bytes_accessed=n * 4_000_000, transcendentals=n * 2_000_000
            ),
            name="attend",
        )(steps, live, q_ids, k_ids, q_own, q_partner, *[slabs[k] for k in chunk], *state)
    ml, acc, message = state
    theirs = hop(message, "y")

    o_packed = pl.pallas_call(
        merge_kernel,
        out_shape=jax.ShapeDtypeStruct((1024, 512), BF),
        in_specs=[VMEM] * 4,
        out_specs=VMEM,
        scratch_shapes=[pltpu.VMEM((CAP, 512), BF)],
        compiler_params=params(24),
        name="merge",
    )(pos[:, None], ml, acc, theirs)

    o_got = lax.all_to_all(o_packed, "ctx", 0, 0, tiled=True)
    o_home = pl.pallas_call(
        home_kernel,
        out_shape=jax.ShapeDtypeStruct((ROWS, 1024), BF),
        in_specs=[SMEM, VMEM],
        out_specs=VMEM,
        compiler_params=params(16),
        name="home",
    )(rot, o_got.reshape(32, 2, 16, 512))
    o_other = lax.ppermute(o_home, "head", [(0, 1), (1, 0)])

    cols = 512
    steps = half_w // cols
    return pl.pallas_call(
        project_kernel,
        out_shape=jax.ShapeDtypeStruct((ROWS, half_w), BF),
        grid_spec=pltpu.PrefetchScalarGridSpec(
            num_scalar_prefetch=1,
            grid=(steps,),
            in_specs=[
                pl.BlockSpec((ROWS, 1024), lambda i, h: (0, 0)),
                pl.BlockSpec((ROWS, 1024), lambda i, h: (0, 0)),
                pl.BlockSpec((1024, cols), lambda i, h: (0, h[0] * steps + i)),
                pl.BlockSpec((1024, cols), lambda i, h: (0, i)),
                pl.BlockSpec((ROWS, 1), lambda i, h: (0, 0)),
            ],
            out_specs=pl.BlockSpec((ROWS, cols), lambda i, h: (0, i)),
        ),
        compiler_params=params(56),
        name="project",
    )(hd.reshape(1), o_home, o_other, weight, w_other, gain)


def solution(mesh):
    return jax.shard_map(
        local,
        mesh=mesh,
        in_specs=(
            P("ctx", "head"),
            P("ctx", "head"),
            P("ctx", "head"),
            P("head", None),
            P("ctx"),
            P("ctx"),
            P("ctx"),
        ),
        out_specs=P("ctx", "head"),
        check_vma=False,
    )
```

```python
import functools

import jax
import jax.numpy as jnp
import numpy as np
from jax import lax
from jax.experimental import pallas as pl
from jax.experimental.pallas import tpu as pltpu
from jax.sharding import PartitionSpec as P

HEAD_WIDTH = 128
THETA = 500000.0
CAP = 320
SLOTS = 8
SHARDS = 128
ROWS = 512
T = 64
N = CAP // T
TILES = N + 1
REACH = (80, 144, 208, 272, 272, 272)
MORE = 16
BIG = float(1 << 30)
LOW = -1e30
EXTRA = 16
BF = jnp.bfloat16
F32 = jnp.float32
SCALE2 = float(1.0 / np.sqrt(128.0) * np.log2(np.e))
VMEM = pl.BlockSpec(memory_space=pltpu.VMEM)
SMEM = pl.BlockSpec(memory_space=pltpu.SMEM)


def params(mib):
    return pltpu.CompilerParams(vmem_limit_bytes=mib * 2**20)


def perm_of(axis, k):
    pairs = []
    for d in range(SHARDS):
        z, x, y = d // 16, d // 4 % 4, d % 4
        if axis == "z":
            z = (z + k) % 8
        elif axis == "x":
            x = (x + k) % 4
        else:
            y = y ^ 1
        pairs.append((d, z * 16 + x * 4 + y))
    return pairs


def hop(a, axis, k=1):
    return lax.ppermute(a, "ctx", perm_of(axis, k))


def ring(a, axis, size, row_dim):
    half = a.shape[row_dim] // 2
    out, up, down = [a], a, a
    for _ in range(size // 2 - 1):
        up, down = hop(up, axis, 1), hop(down, axis, -1)
        out += [up, down]
    lo = hop(lax.slice_in_dim(up, 0, half, axis=row_dim), axis, 1)
    hi = hop(lax.slice_in_dim(down, half, 2 * half, axis=row_dim), axis, -1)
    out.append(jnp.concatenate([lo, hi], axis=row_dim))
    return out


def ring_steps(size):
    steps = [0]
    for i in range(1, size // 2):
        steps += [-i, i]
    return steps + [size // 2]


def pack_matrix(rot, transpose):
    packed_dim = 1 if transpose else 0
    o = lax.broadcasted_iota(jnp.int32, (ROWS, ROWS), packed_dim)
    s = lax.broadcasted_iota(jnp.int32, (ROWS, ROWS), 1 - packed_dim)
    src = (o & 7) * 64 + (((o >> 3) + 64 - rot) & 63)
    return jnp.where(src == s, 1.0, 0.0).astype(BF)


def pack_kernel(rot_ref, q_ref, k_ref, v_ref, cos_ref, sin_ref, out_ref):
    cos, sin = cos_ref[...], sin_ref[...]

    def rotate(x):
        x = x.astype(F32)
        return (x * cos + pltpu.roll(x, 64, 1) * sin).astype(BF)

    m = pack_matrix(rot_ref[0], False)
    parts = [rotate(q_ref[:, g * 128 : (g + 1) * 128]) for g in range(4)]
    parts += [rotate(k_ref[...]), v_ref[...]]
    for c, x in enumerate(parts):
        y = jnp.dot(m, x, preferred_element_type=F32).astype(BF)
        out_ref[:, 0, :, c * 128 : (c + 1) * 128] = y.reshape(32, 16, 128)


def compact_matrix(pos):
    p = lax.broadcasted_iota(jnp.int32, (CAP, SHARDS * SLOTS), 0)
    return jnp.where(p == pos, 1.0, 0.0).astype(BF)


def columns(i):
    if i < N - 1:
        return [(i * T, T, g) for g in range(4)]
    return [(i * T + b * 32, 32, g) for b in range(2) for g in range(4)]


def compact_kernel(pos_ref, x_ref, kv_ref, q_ref):
    m = compact_matrix(pos_ref[...])
    kv_ref[...] = jnp.dot(m, x_ref[:, 512:], preferred_element_type=F32).astype(BF)
    y = jnp.dot(m, x_ref[:, :512], preferred_element_type=F32).astype(BF)
    for i in range(N):
        at = 0
        for row, rows, g in columns(i):
            q_ref[i, at : at + rows, :] = y[row : row + rows, g * 128 : (g + 1) * 128]
            at += rows


def attend_kernel(n, first, last, halves, *refs):
    more_ref, live_ref, qid_ref, kid_ref, qa_ref, qb_ref = refs[:6]
    kv_refs, refs = refs[6 : 6 + n], refs[6 + n :]
    if not first:
        refs = refs[2:]
    ml_ref, acc_ref = refs[:2]
    if first:
        row = lax.broadcasted_iota(jnp.int32, ml_ref.shape, 2)
        ml_ref[...] = jnp.where(row == 0, LOW, 0.0)
        acc_ref[...] = jnp.zeros_like(acc_ref)

    def batch(tiles, start, rows):
        at = pl.ds(start, rows)
        keys = [kv[:, at, :128].reshape(4 * rows, 128) for kv in kv_refs]
        vals = [kv[:, at, 128:].reshape(4 * rows, 128) for kv in kv_refs]
        kids = []
        for c in range(n):
            col = kid_ref[c, :, at, :].reshape(4 * rows, 128)
            kids.append(jnp.concatenate([col, col], axis=1))
        old = [(ml_ref[h, i, 0:1, :], ml_ref[h, i, 1:2, :], acc_ref[h, i]) for _, _, h, i in tiles]
        found = []
        for (q, qid, _, _), (m, _, _) in zip(tiles, old):
            scores = []
            for key, kid in zip(keys, kids):
                s = lax.dot_general(key, q, (((1,), (1,)), ((), ())), preferred_element_type=F32)
                s = jnp.where(kid <= qid, s, LOW)
                m = jnp.maximum(m, jnp.max(s, axis=0, keepdims=True))
                scores.append(s)
            found.append((scores, m))
        done = []
        for (scores, new), (m, total, acc) in zip(found, old):
            keep = jnp.exp2((m - new) * SCALE2)
            total, acc = total * keep, acc * keep
            for s, val in zip(scores, vals):
                p = jnp.exp2((s - new) * SCALE2)
                total = total + jnp.sum(p, axis=0, keepdims=True)
                acc = acc + lax.dot_general(
                    val, p.astype(BF), (((0,), (0,)), ((), ())), preferred_element_type=F32
                )
            done.append((new, total, acc))
        for (_, _, h, i), (m, total, acc) in zip(tiles, done):
            ml_ref[h, i, 0:1, :] = m
            ml_ref[h, i, 1:2, :] = total
            acc_ref[h, i] = acc

    def visit(i):
        if i < N - 1:
            q = (qa_ref, qb_ref)
            tiles = [(q[h][i], qid_ref[h, i], h, i) for h in halves]
        else:
            b = i - (N - 1)
            c = slice(b * 128, (b + 1) * 128)
            q = jnp.concatenate([qa_ref[N - 1, c], qb_ref[N - 1, c]], axis=0)
            qid = jnp.concatenate([qid_ref[0, N - 1, :, c], qid_ref[1, N - 1, :, c]], axis=1)
            tiles = [(q, qid, b, N - 1)]
        batch(tiles, 0, REACH[i])

        def further(e, _):
            batch(tiles, pl.multiple_of(REACH[i] + e * MORE, MORE), MORE)
            return 0

        lax.fori_loop(0, more_ref[i], further, 0)

    for i in range(TILES):
        if i < N - 1:
            visit(i)
        elif 1 in halves:
            pl.when(live_ref[i] > 0)(functools.partial(visit, i))
    if last:
        for i in range(N):
            o, lse = of_half(1, i, ml_ref, acc_ref)
            hi = lse.astype(BF).astype(F32)
            mid = (lse - hi).astype(BF).astype(F32)
            lo = lse - hi - mid
            row = lax.broadcasted_iota(jnp.int32, (EXTRA, 4 * T), 0)
            note = jnp.where(row == 0, hi, jnp.where(row == 1, mid, jnp.where(row == 2, lo, 0.0)))
            refs[2][i, :128, :] = o.astype(BF)
            refs[2][i, 128:, :] = note.astype(BF)


def of_half(half, i, ml_ref, acc_ref):
    if i < N - 1:
        return finish(ml_ref[half, i], acc_ref[half, i])
    c = slice(half * 128, (half + 1) * 128)
    ml = jnp.concatenate([ml_ref[0, i, :, c], ml_ref[1, i, :, c]], axis=1)
    acc = jnp.concatenate([acc_ref[0, i, :, c], acc_ref[1, i, :, c]], axis=1)
    return finish(ml, acc)


def finish(ml, acc):
    m, total = ml[0:1], ml[1:2]
    some = total > 0.0
    total = jnp.where(some, total, 1.0)
    lse = jnp.where(some, m * SCALE2 + jnp.log2(total), LOW)
    return acc / total, lse


def merge_kernel(post_ref, ml_ref, acc_ref, got_ref, out_ref, ob_ref):
    for i in range(N):
        mine, lse_a = of_half(0, i, ml_ref, acc_ref)
        got = got_ref[i].astype(F32)
        lse_b = got[128:129] + got[129:130] + got[130:131]
        top = jnp.maximum(lse_a, lse_b)
        wa, wb = jnp.exp2(lse_a - top), jnp.exp2(lse_b - top)
        inv = 1.0 / (wa + wb)
        o = (mine * (wa * inv) + got[:128] * (wb * inv)).T.astype(BF)
        at = 0
        for row, rows, g in columns(i):
            ob_ref[row : row + rows, g * 128 : (g + 1) * 128] = o[at : at + rows]
            at += rows
    p = lax.broadcasted_iota(jnp.int32, (SHARDS * SLOTS, CAP), 1)
    spread = jnp.where(p == post_ref[...], 1.0, 0.0).astype(BF)
    out_ref[...] = jnp.dot(spread, ob_ref[...], preferred_element_type=F32).astype(BF)


def home_kernel(rot_ref, o_ref, out_ref):
    m = pack_matrix(rot_ref[0], True)
    for h in range(2):
        x = o_ref[:, h, :, :].reshape(ROWS, 512)
        out_ref[:, h * 512 : (h + 1) * 512] = jnp.dot(m, x, preferred_element_type=F32).astype(BF)


def project_kernel(at_ref, own_ref, got_ref, wa_ref, wb_ref, gain_ref, out_ref, other_ref):
    @pl.when(pl.program_id(0) == 0)
    def _():
        m = pack_matrix(at_ref[1], True)
        for h in range(2):
            x = got_ref[:, h, :, :].reshape(ROWS, 512)
            y = jnp.dot(m, x, preferred_element_type=F32).astype(BF)
            other_ref[:, h * 512 : (h + 1) * 512] = y

    s = jnp.dot(own_ref[...], wa_ref[...], preferred_element_type=F32)
    s = s + jnp.dot(other_ref[...], wb_ref[...], preferred_element_type=F32)
    s = s.astype(BF).astype(F32)
    gain = gain_ref[:, :1]
    out_ref[...] = jnp.where(gain != 0.0, gain * s, 0.0).astype(BF)


def local(q_home, k_home, v_home, weight, router, positions, counts):
    d = lax.axis_index("ctx").astype(jnp.int32)
    hd = lax.axis_index("head").astype(jnp.int32)
    half_w = weight.shape[1] // 2

    to_send = lax.dynamic_slice_in_dim(weight, (1 - hd) * half_w, half_w, axis=1)
    w_other = lax.ppermute(to_send, "head", [(0, 1), (1, 0)])

    freqs = THETA ** (-(jnp.arange(64, dtype=F32) * 2.0 / HEAD_WIDTH))
    angles = positions.astype(F32)[:, None] * jnp.concatenate([freqs, freqs])[None, :]
    sign = jnp.where(jnp.arange(128) < 64, -1.0, 1.0).astype(F32)
    cos, sin = jnp.cos(angles), jnp.sin(angles) * sign[None, :]
    rot = (d % 64).reshape(1)

    packed = pl.pallas_call(
        pack_kernel,
        out_shape=jax.ShapeDtypeStruct((32, 2, 16, 768), BF),
        grid=(2,),
        in_specs=[
            SMEM,
            pl.BlockSpec((ROWS, 512), lambda h: (0, h)),
            pl.BlockSpec((ROWS, 128), lambda h: (0, h)),
            pl.BlockSpec((ROWS, 128), lambda h: (0, h)),
            pl.BlockSpec((ROWS, 128), lambda h: (0, 0)),
            pl.BlockSpec((ROWS, 128), lambda h: (0, 0)),
        ],
        out_specs=pl.BlockSpec((32, 1, 16, 768), lambda h: (0, h, 0, 0)),
        compiler_params=params(56),
        name="pack",
    )(rot, q_home, k_home, v_home, cos, sin)
    got = lax.all_to_all(packed.reshape(1024, 768), "ctx", 0, 0, tiled=True)
    all_counts = lax.all_gather(counts, "ctx", axis=0, tiled=True)

    z, x, yl = d // 16, d // 4 % 4, d % 2
    dz = jnp.asarray(np.array(ring_steps(8), np.int32))
    dx = jnp.asarray(np.array(ring_steps(4), np.int32))
    member = ((z + dz) % 8)[:, None] * 8 + ((x + dx) % 4)[None, :] * 2 + yl
    partner = z * 8 + x * 2 + (1 - yl)
    member = jnp.concatenate([member.reshape(32), partner.reshape(1)])
    shard = jnp.arange(SHARDS, dtype=jnp.int32)

    def layout(who, all_counts):
        offset = (who[:, None] - shard[None, :]) % 64
        held = jnp.maximum((all_counts[None, :] - offset + 63) // 64, 0)
        before = (shard[:, None] < shard[None, :]).astype(BF)
        start = jnp.dot(held.astype(BF), before, preferred_element_type=F32).astype(jnp.int32)
        return offset, held, start

    _, held, start = layout(member[:1], all_counts)
    slot = jnp.arange(SLOTS, dtype=jnp.int32)[None, :]
    pos = jnp.where(slot < held[0][:, None], start[0][:, None] + slot, -1).reshape(-1)
    kv_own, q_own = pl.pallas_call(
        compact_kernel,
        out_shape=(
            jax.ShapeDtypeStruct((CAP, 256), BF),
            jax.ShapeDtypeStruct((N, 4 * T, 128), BF),
        ),
        in_specs=[VMEM] * 2,
        out_specs=(VMEM, VMEM),
        compiler_params=params(16),
        name="compact",
    )(pos[None, :], got)
    kv_own, q_own, counts_now = lax.optimization_barrier((kv_own, q_own, all_counts))
    q_partner = hop(q_own, "y")
    slab = jnp.stack([kv_own, hop(kv_own, "x", 1), hop(kv_own, "x", -1), hop(kv_own, "x", 2)])
    own_live = jnp.arange(ROWS, dtype=jnp.int32) < counts[0]
    gain = jnp.broadcast_to(jnp.where(own_live, router, 0.0)[:, None], (ROWS, 128))
    slab, q_partner, gain = lax.optimization_barrier((slab, q_partner, gain))
    slabs = ring(slab, "z", 8, 1)

    offset, held, start = layout(member, counts_now)
    base = (shard[None, :] * ROWS + offset - 64 * start).astype(F32)
    place = jnp.arange(CAP, dtype=jnp.int32)[None, None, :]
    inside = (start[:, :, None] <= place) & (place < (start + held)[:, :, None])
    ids = jnp.sum(jnp.where(inside, base[:, :, None] + (64 * place).astype(F32), 0.0), axis=1)
    ids = jnp.where(place[0] < jnp.sum(held, axis=1)[:, None], ids, BIG)
    q_rows = jnp.stack([ids[0], ids[32]])
    best = jnp.max(jnp.where(q_rows >= BIG, -1.0, q_rows), axis=0)
    tile_of = np.minimum(np.arange(CAP) // T, N - 1) + (np.arange(CAP) >= CAP - 32)
    here = jnp.asarray(tile_of[None, :] == np.arange(TILES)[:, None])
    q_max = jnp.max(jnp.where(here, best[None, :], -1.0), axis=1)
    live = (q_max >= 0.0).astype(jnp.int32)
    reach = jnp.sum((ids[:32, None, :] <= q_max[None, :, None]).astype(jnp.int32), axis=2)
    reach = jnp.max(reach.reshape(8, 4, TILES), axis=1)
    more = jnp.maximum(reach - jnp.asarray(REACH, jnp.int32)[None, :] + MORE - 1, 0) // MORE
    q_tiles = q_rows[:, : CAP - T].reshape(2, N - 1, 1, T)
    q_ids = jnp.tile(q_tiles[:, :, :, :], (1, 1, 4, 1)).reshape(2, N - 1, 1, 4 * T)
    q_last = jnp.tile(q_rows[:, CAP - T :].reshape(2, 2, 1, 32), (1, 1, 4, 1))
    q_ids = jnp.concatenate([q_ids, q_last.reshape(2, 1, 1, 4 * T)], axis=1)
    slab_ids = ids[:32].reshape(8, 4, CAP, 1)

    state = ()
    both = (0, 1)
    calls = (((0,), both), ((1, 2), both), ((3, 4), both), ((5, 6), both), ((7,), (1,)), ((7,), (0,)))
    for c, (chunk, halves) in enumerate(calls):
        first, last, n = c == 0, halves == (1,), len(chunk)
        steps = jnp.max(more[chunk[0] : chunk[-1] + 1], axis=0)
        k_ids = jnp.broadcast_to(slab_ids[chunk[0] : chunk[-1] + 1], (n, 4, CAP, 128))
        shapes = [
            jax.ShapeDtypeStruct((2, N, 8, 4 * T), F32),
            jax.ShapeDtypeStruct((2, N, 128, 4 * T), F32),
        ]
        if last:
            shapes.append(jax.ShapeDtypeStruct((N, 128 + EXTRA, 4 * T), BF))
        state = pl.pallas_call(
            functools.partial(attend_kernel, n, first, last, halves),
            out_shape=tuple(shapes),
            in_specs=[SMEM] * 2 + [VMEM] * (4 + n + len(state)),
            out_specs=(VMEM,) * len(shapes),
            input_output_aliases={} if first else {6 + n: 0, 7 + n: 1},
            compiler_params=params(48),
            cost_estimate=pl.CostEstimate(
                flops=n * 4_000_000_000, bytes_accessed=n * 4_000_000, transcendentals=n * 2_000_000
            ),
            name="attend",
        )(steps, live, q_ids, k_ids, q_own, q_partner, *[slabs[k] for k in chunk], *state)
        if last:
            theirs = hop(state[2], "y")
            state = state[:2]
    ml, acc = state

    o_packed = pl.pallas_call(
        merge_kernel,
        out_shape=jax.ShapeDtypeStruct((1024, 512), BF),
        in_specs=[VMEM] * 4,
        out_specs=VMEM,
        scratch_shapes=[pltpu.VMEM((CAP, 512), BF)],
        compiler_params=params(24),
        name="merge",
    )(pos[:, None], ml, acc, theirs)

    o_got = lax.all_to_all(o_packed, "ctx", 0, 0, tiled=True)
    o_far = lax.ppermute(o_got, "head", [(0, 1), (1, 0)])
    o_home = pl.pallas_call(
        home_kernel,
        out_shape=jax.ShapeDtypeStruct((ROWS, 1024), BF),
        in_specs=[SMEM, VMEM],
        out_specs=VMEM,
        compiler_params=params(16),
        name="home",
    )(rot, o_got.reshape(32, 2, 16, 512))

    cols = 512
    steps = half_w // cols
    return pl.pallas_call(
        project_kernel,
        out_shape=jax.ShapeDtypeStruct((ROWS, half_w), BF),
        grid_spec=pltpu.PrefetchScalarGridSpec(
            num_scalar_prefetch=1,
            grid=(steps,),
            in_specs=[
                pl.BlockSpec((ROWS, 1024), lambda i, h: (0, 0)),
                pl.BlockSpec((32, 2, 16, 512), lambda i, h: (0, 0, 0, 0)),
                pl.BlockSpec((1024, cols), lambda i, h: (0, h[0] * steps + i)),
                pl.BlockSpec((1024, cols), lambda i, h: (0, i)),
                pl.BlockSpec((ROWS, 128), lambda i, h: (0, 0)),
            ],
            out_specs=pl.BlockSpec((ROWS, cols), lambda i, h: (0, i)),
            scratch_shapes=[pltpu.VMEM((ROWS, 1024), BF)],
        ),
        compiler_params=params(56),
        name="project",
    )(
        jnp.concatenate([hd.reshape(1), rot]),
        o_home,
        o_far.reshape(32, 2, 16, 512),
        weight,
        w_other,
        gain,
    )


def solution(mesh):
    return jax.shard_map(
        local,
        mesh=mesh,
        in_specs=(
            P("ctx", "head"),
            P("ctx", "head"),
            P("ctx", "head"),
            P("head", None),
            P("ctx"),
            P("ctx"),
            P("ctx"),
        ),
        out_specs=P("ctx", "head"),
        check_vma=False,
    )
```

```python
import functools

import jax
import jax.numpy as jnp
import numpy as np
from jax import lax
from jax.experimental import pallas as pl
from jax.experimental.pallas import tpu as pltpu
from jax.sharding import PartitionSpec as P

HEAD_WIDTH = 128
THETA = 500000.0
CAP = 320
SLOTS = 8
SHARDS = 128
ROWS = 512
T = 64
N = CAP // T
TILES = N + 1
REACH = (80, 144, 208, 272, 272, 272)
MORE = 16
BIG = float(1 << 30)
LOW = -1e30
EXTRA = 16
BF = jnp.bfloat16
F32 = jnp.float32
SCALE2 = float(1.0 / np.sqrt(128.0) * np.log2(np.e))
VMEM = pl.BlockSpec(memory_space=pltpu.VMEM)
SMEM = pl.BlockSpec(memory_space=pltpu.SMEM)


def params(mib):
    return pltpu.CompilerParams(vmem_limit_bytes=mib * 2**20)


def perm_of(axis, k):
    pairs = []
    for d in range(SHARDS):
        z, x, y = d // 16, d // 4 % 4, d % 4
        if axis == "z":
            z = (z + k) % 8
        elif axis == "x":
            x = (x + k) % 4
        else:
            y = y ^ 1
        pairs.append((d, z * 16 + x * 4 + y))
    return pairs


def hop(a, axis, k=1):
    return lax.ppermute(a, "ctx", perm_of(axis, k))


def ring(a, axis, size, row_dim):
    half = a.shape[row_dim] // 2
    out, up, down = [a], a, a
    for _ in range(size // 2 - 1):
        up, down = hop(up, axis, 1), hop(down, axis, -1)
        out += [up, down]
    lo = hop(lax.slice_in_dim(up, 0, half, axis=row_dim), axis, 1)
    hi = hop(lax.slice_in_dim(down, half, 2 * half, axis=row_dim), axis, -1)
    out.append(jnp.concatenate([lo, hi], axis=row_dim))
    return out


def ring_steps(size):
    steps = [0]
    for i in range(1, size // 2):
        steps += [-i, i]
    return steps + [size // 2]


def pack_matrix(rot, transpose):
    packed_dim = 1 if transpose else 0
    o = lax.broadcasted_iota(jnp.int32, (ROWS, ROWS), packed_dim)
    s = lax.broadcasted_iota(jnp.int32, (ROWS, ROWS), 1 - packed_dim)
    src = (o & 7) * 64 + (((o >> 3) + 64 - rot) & 63)
    return jnp.where(src == s, 1.0, 0.0).astype(BF)


def pack_kernel(rot_ref, q_ref, k_ref, v_ref, cos_ref, sin_ref, out_ref):
    cos, sin = cos_ref[...], sin_ref[...]

    def rotate(x):
        x = x.astype(F32)
        return (x * cos + pltpu.roll(x, 64, 1) * sin).astype(BF)

    m = pack_matrix(rot_ref[0], False)
    parts = [rotate(q_ref[:, g * 128 : (g + 1) * 128]) for g in range(4)]
    parts += [rotate(k_ref[...]), v_ref[...]]
    for c, x in enumerate(parts):
        y = jnp.dot(m, x, preferred_element_type=F32).astype(BF)
        out_ref[:, 0, :, c * 128 : (c + 1) * 128] = y.reshape(32, 16, 128)


def compact_matrix(pos):
    p = lax.broadcasted_iota(jnp.int32, (CAP, SHARDS * SLOTS), 0)
    return jnp.where(p == pos, 1.0, 0.0).astype(BF)


def columns(i):
    if i < N - 1:
        return [(i * T, T, g) for g in range(4)]
    return [(i * T + b * 32, 32, g) for b in range(2) for g in range(4)]


def compact_kernel(pos_ref, x_ref, kv_ref, q_ref):
    m = compact_matrix(pos_ref[...])
    kv_ref[...] = jnp.dot(m, x_ref[:, 512:], preferred_element_type=F32).astype(BF)
    y = jnp.dot(m, x_ref[:, :512], preferred_element_type=F32).astype(BF)
    for i in range(N):
        at = 0
        for row, rows, g in columns(i):
            q_ref[i, at : at + rows, :] = y[row : row + rows, g * 128 : (g + 1) * 128]
            at += rows


def attend_kernel(n, first, last, *refs):
    more_ref, live_ref, qid_ref, kid_ref, qa_ref, qb_ref = refs[:6]
    kv_refs, refs = refs[6 : 6 + n], refs[6 + n :]
    if not first:
        refs = refs[2:]
    ml_ref, acc_ref = refs[:2]
    if first:
        row = lax.broadcasted_iota(jnp.int32, ml_ref.shape, 2)
        ml_ref[...] = jnp.where(row == 0, LOW, 0.0)
        acc_ref[...] = jnp.zeros_like(acc_ref)

    def batch(tiles, start, rows):
        at = pl.ds(start, rows)
        keys = [kv[:, at, :128].reshape(4 * rows, 128) for kv in kv_refs]
        vals = [kv[:, at, 128:].reshape(4 * rows, 128) for kv in kv_refs]
        kids = []
        for c in range(n):
            col = kid_ref[c, :, at, :].reshape(4 * rows, 128)
            kids.append(jnp.concatenate([col, col], axis=1))
        old = [(ml_ref[h, i, 0:1, :], ml_ref[h, i, 1:2, :], acc_ref[h, i]) for _, _, h, i in tiles]
        found = []
        for (q, qid, _, _), (m, _, _) in zip(tiles, old):
            scores = []
            for key, kid in zip(keys, kids):
                s = lax.dot_general(key, q, (((1,), (1,)), ((), ())), preferred_element_type=F32)
                s = jnp.where(kid <= qid, s, LOW)
                m = jnp.maximum(m, jnp.max(s, axis=0, keepdims=True))
                scores.append(s)
            found.append((scores, m))
        done = []
        for (scores, new), (m, total, acc) in zip(found, old):
            keep = jnp.exp2((m - new) * SCALE2)
            total, acc = total * keep, acc * keep
            for s, val in zip(scores, vals):
                p = jnp.exp2((s - new) * SCALE2)
                total = total + jnp.sum(p, axis=0, keepdims=True)
                acc = acc + lax.dot_general(
                    val, p.astype(BF), (((0,), (0,)), ((), ())), preferred_element_type=F32
                )
            done.append((new, total, acc))
        for (_, _, h, i), (m, total, acc) in zip(tiles, done):
            ml_ref[h, i, 0:1, :] = m
            ml_ref[h, i, 1:2, :] = total
            acc_ref[h, i] = acc

    def visit(i):
        if i < N - 1:
            tiles = [(qa_ref[i], qid_ref[0, i], 0, i), (qb_ref[i], qid_ref[1, i], 1, i)]
        else:
            b = i - (N - 1)
            c = slice(b * 128, (b + 1) * 128)
            q = jnp.concatenate([qa_ref[N - 1, c], qb_ref[N - 1, c]], axis=0)
            qid = jnp.concatenate([qid_ref[0, N - 1, :, c], qid_ref[1, N - 1, :, c]], axis=1)
            tiles = [(q, qid, b, N - 1)]
        batch(tiles, 0, REACH[i])

        def further(e, _):
            batch(tiles, pl.multiple_of(REACH[i] + e * MORE, MORE), MORE)
            return 0

        lax.fori_loop(0, more_ref[i], further, 0)

    for i in range(TILES):
        if i < N - 1:
            visit(i)
        else:
            pl.when(live_ref[i] > 0)(functools.partial(visit, i))
    if last:
        for i in range(N):
            o, lse = of_half(1, i, ml_ref, acc_ref)
            hi = lse.astype(BF).astype(F32)
            mid = (lse - hi).astype(BF).astype(F32)
            lo = lse - hi - mid
            row = lax.broadcasted_iota(jnp.int32, (EXTRA, 4 * T), 0)
            note = jnp.where(row == 0, hi, jnp.where(row == 1, mid, jnp.where(row == 2, lo, 0.0)))
            refs[2][i, :128, :] = o.astype(BF)
            refs[2][i, 128:, :] = note.astype(BF)


def of_half(half, i, ml_ref, acc_ref):
    if i < N - 1:
        return finish(ml_ref[half, i], acc_ref[half, i])
    c = slice(half * 128, (half + 1) * 128)
    ml = jnp.concatenate([ml_ref[0, i, :, c], ml_ref[1, i, :, c]], axis=1)
    acc = jnp.concatenate([acc_ref[0, i, :, c], acc_ref[1, i, :, c]], axis=1)
    return finish(ml, acc)


def finish(ml, acc):
    m, total = ml[0:1], ml[1:2]
    some = total > 0.0
    total = jnp.where(some, total, 1.0)
    lse = jnp.where(some, m * SCALE2 + jnp.log2(total), LOW)
    return acc / total, lse


def merge_kernel(post_ref, ml_ref, acc_ref, got_ref, out_ref, ob_ref):
    for i in range(N):
        mine, lse_a = of_half(0, i, ml_ref, acc_ref)
        got = got_ref[i].astype(F32)
        lse_b = got[128:129] + got[129:130] + got[130:131]
        top = jnp.maximum(lse_a, lse_b)
        wa, wb = jnp.exp2(lse_a - top), jnp.exp2(lse_b - top)
        inv = 1.0 / (wa + wb)
        o = (mine * (wa * inv) + got[:128] * (wb * inv)).T.astype(BF)
        at = 0
        for row, rows, g in columns(i):
            ob_ref[row : row + rows, g * 128 : (g + 1) * 128] = o[at : at + rows]
            at += rows
    p = lax.broadcasted_iota(jnp.int32, (SHARDS * SLOTS, CAP), 1)
    spread = jnp.where(p == post_ref[...], 1.0, 0.0).astype(BF)
    out_ref[...] = jnp.dot(spread, ob_ref[...], preferred_element_type=F32).astype(BF)


def home_kernel(rot_ref, o_ref, out_ref):
    m = pack_matrix(rot_ref[0], True)
    for h in range(2):
        x = o_ref[:, h, :, :].reshape(ROWS, 512)
        out_ref[:, h * 512 : (h + 1) * 512] = jnp.dot(m, x, preferred_element_type=F32).astype(BF)


def project_kernel(
    hd_ref, own_ref, other_ref, wa_ref, wb_ref, gain_ref, out_ref, a_ref, b_ref, o_ref, sems
):
    n, cols = o_ref.shape[0], o_ref.shape[2]
    first = pl.multiple_of(hd_ref[0] * (n * cols), n * cols)
    loads = []
    for i in range(n):
        mine = wa_ref.at[:, pl.ds(first + i * cols, cols)]
        a = pltpu.make_async_copy(mine, a_ref.at[i], sems.at[0, i])
        theirs = wb_ref.at[:, pl.ds(i * cols, cols)]
        b = pltpu.make_async_copy(theirs, b_ref.at[i], sems.at[1, i])
        a.start()
        b.start()
        loads.append((a, b))
    gain = gain_ref[:, :1]
    stores = []
    for i, (a, b) in enumerate(loads):
        a.wait()
        s = jnp.dot(own_ref[...], a_ref[i], preferred_element_type=F32)
        b.wait()
        s = s + jnp.dot(other_ref[...], b_ref[i], preferred_element_type=F32)
        s = s.astype(BF).astype(F32)
        o_ref[i] = jnp.where(gain != 0.0, gain * s, 0.0).astype(BF)
        out = out_ref.at[:, pl.ds(i * cols, cols)]
        store = pltpu.make_async_copy(o_ref.at[i], out, sems.at[2, i])
        store.start()
        stores.append(store)
    for store in stores:
        store.wait()


def local(q_home, k_home, v_home, weight, router, positions, counts):
    d = lax.axis_index("ctx").astype(jnp.int32)
    hd = lax.axis_index("head").astype(jnp.int32)
    half_w = weight.shape[1] // 2

    to_send = lax.dynamic_slice_in_dim(weight, (1 - hd) * half_w, half_w, axis=1)
    own_live = jnp.arange(ROWS, dtype=jnp.int32) < counts[0]
    gain = jnp.broadcast_to(jnp.where(own_live, router, 0.0)[:, None], (ROWS, 128))
    to_send, gain = lax.optimization_barrier((to_send, gain))
    w_other = lax.ppermute(to_send, "head", [(0, 1), (1, 0)])

    freqs = THETA ** (-(jnp.arange(64, dtype=F32) * 2.0 / HEAD_WIDTH))
    angles = positions.astype(F32)[:, None] * jnp.concatenate([freqs, freqs])[None, :]
    sign = jnp.where(jnp.arange(128) < 64, -1.0, 1.0).astype(F32)
    cos, sin = jnp.cos(angles), jnp.sin(angles) * sign[None, :]
    rot = (d % 64).reshape(1)

    packed = pl.pallas_call(
        pack_kernel,
        out_shape=jax.ShapeDtypeStruct((32, 2, 16, 768), BF),
        grid=(2,),
        in_specs=[
            SMEM,
            pl.BlockSpec((ROWS, 512), lambda h: (0, h)),
            pl.BlockSpec((ROWS, 128), lambda h: (0, h)),
            pl.BlockSpec((ROWS, 128), lambda h: (0, h)),
            pl.BlockSpec((ROWS, 128), lambda h: (0, 0)),
            pl.BlockSpec((ROWS, 128), lambda h: (0, 0)),
        ],
        out_specs=pl.BlockSpec((32, 1, 16, 768), lambda h: (0, h, 0, 0)),
        compiler_params=params(56),
        name="pack",
    )(rot, q_home, k_home, v_home, cos, sin)
    got = lax.all_to_all(packed.reshape(1024, 768), "ctx", 0, 0, tiled=True)
    all_counts = lax.all_gather(counts, "ctx", axis=0, tiled=True)

    z, x, yl = d // 16, d // 4 % 4, d % 2
    dz = jnp.asarray(np.array(ring_steps(8), np.int32))
    dx = jnp.asarray(np.array(ring_steps(4), np.int32))
    member = ((z + dz) % 8)[:, None] * 8 + ((x + dx) % 4)[None, :] * 2 + yl
    partner = z * 8 + x * 2 + (1 - yl)
    member = jnp.concatenate([member.reshape(32), partner.reshape(1)])
    shard = jnp.arange(SHARDS, dtype=jnp.int32)

    def layout(who, all_counts):
        offset = (who[:, None] - shard[None, :]) % 64
        held = jnp.maximum((all_counts[None, :] - offset + 63) // 64, 0)
        before = (shard[:, None] < shard[None, :]).astype(BF)
        start = jnp.dot(held.astype(BF), before, preferred_element_type=F32).astype(jnp.int32)
        return offset, held, start

    _, held, start = layout(member[:1], all_counts)
    slot = jnp.arange(SLOTS, dtype=jnp.int32)[None, :]
    pos = jnp.where(slot < held[0][:, None], start[0][:, None] + slot, -1).reshape(-1)
    kv_own, q_own = pl.pallas_call(
        compact_kernel,
        out_shape=(
            jax.ShapeDtypeStruct((CAP, 256), BF),
            jax.ShapeDtypeStruct((N, 4 * T, 128), BF),
        ),
        in_specs=[VMEM] * 2,
        out_specs=(VMEM, VMEM),
        compiler_params=params(16),
        name="compact",
    )(pos[None, :], got)
    kv_own, q_own, counts_now = lax.optimization_barrier((kv_own, q_own, all_counts))
    q_partner = hop(q_own, "y")
    slab = jnp.stack(ring(kv_own, "x", 4, 0))
    slab, q_partner = lax.optimization_barrier((slab, q_partner))
    slabs = ring(slab, "z", 8, 1)

    offset, held, start = layout(member, counts_now)
    base = (shard[None, :] * ROWS + offset - 64 * start).astype(F32)
    place = jnp.arange(CAP, dtype=jnp.int32)[None, None, :]
    inside = (start[:, :, None] <= place) & (place < (start + held)[:, :, None])
    ids = jnp.sum(jnp.where(inside, base[:, :, None] + (64 * place).astype(F32), 0.0), axis=1)
    ids = jnp.where(place[0] < jnp.sum(held, axis=1)[:, None], ids, BIG)
    q_rows = jnp.stack([ids[0], ids[32]])
    best = jnp.max(jnp.where(q_rows >= BIG, -1.0, q_rows), axis=0)
    tile_of = np.minimum(np.arange(CAP) // T, N - 1) + (np.arange(CAP) >= CAP - 32)
    here = jnp.asarray(tile_of[None, :] == np.arange(TILES)[:, None])
    q_max = jnp.max(jnp.where(here, best[None, :], -1.0), axis=1)
    live = (q_max >= 0.0).astype(jnp.int32)
    reach = jnp.sum((ids[:32, None, :] <= q_max[None, :, None]).astype(jnp.int32), axis=2)
    reach = jnp.max(reach.reshape(8, 4, TILES), axis=1)
    more = jnp.maximum(reach - jnp.asarray(REACH, jnp.int32)[None, :] + MORE - 1, 0) // MORE
    q_tiles = q_rows[:, : CAP - T].reshape(2, N - 1, 1, T)
    q_ids = jnp.tile(q_tiles[:, :, :, :], (1, 1, 4, 1)).reshape(2, N - 1, 1, 4 * T)
    q_last = jnp.tile(q_rows[:, CAP - T :].reshape(2, 2, 1, 32), (1, 1, 4, 1))
    q_ids = jnp.concatenate([q_ids, q_last.reshape(2, 1, 1, 4 * T)], axis=1)
    slab_ids = ids[:32].reshape(8, 4, CAP, 1)

    state = ()
    chunks = ((0,), (1, 2), (3, 4), (5, 6), (7,))
    for c, chunk in enumerate(chunks):
        first, last, n = c == 0, c == len(chunks) - 1, len(chunk)
        steps = jnp.max(more[chunk[0] : chunk[-1] + 1], axis=0)
        k_ids = jnp.broadcast_to(slab_ids[chunk[0] : chunk[-1] + 1], (n, 4, CAP, 128))
        shapes = [
            jax.ShapeDtypeStruct((2, N, 8, 4 * T), F32),
            jax.ShapeDtypeStruct((2, N, 128, 4 * T), F32),
        ]
        if last:
            shapes.append(jax.ShapeDtypeStruct((N, 128 + EXTRA, 4 * T), BF))
        state = pl.pallas_call(
            functools.partial(attend_kernel, n, first, last),
            out_shape=tuple(shapes),
            in_specs=[SMEM] * 2 + [VMEM] * (4 + n + len(state)),
            out_specs=(VMEM,) * len(shapes),
            input_output_aliases={} if first else {6 + n: 0, 7 + n: 1},
            compiler_params=params(48),
            cost_estimate=pl.CostEstimate(
                flops=n * 4_000_000_000, bytes_accessed=n * 4_000_000, transcendentals=n * 2_000_000
            ),
            name="attend",
        )(steps, live, q_ids, k_ids, q_own, q_partner, *[slabs[k] for k in chunk], *state)
    ml, acc, message = state
    theirs = hop(message, "y")

    o_packed = pl.pallas_call(
        merge_kernel,
        out_shape=jax.ShapeDtypeStruct((1024, 512), BF),
        in_specs=[VMEM] * 4,
        out_specs=VMEM,
        scratch_shapes=[pltpu.VMEM((CAP, 512), BF)],
        compiler_params=params(24),
        name="merge",
    )(pos[:, None], ml, acc, theirs)

    o_got = lax.all_to_all(o_packed, "ctx", 0, 0, tiled=True)
    o_home = pl.pallas_call(
        home_kernel,
        out_shape=jax.ShapeDtypeStruct((ROWS, 1024), BF),
        in_specs=[SMEM, VMEM],
        out_specs=VMEM,
        compiler_params=params(16),
        name="home",
    )(rot, o_got.reshape(32, 2, 16, 512))
    o_other = lax.ppermute(o_home, "head", [(0, 1), (1, 0)])

    cols = 512
    steps = half_w // cols
    hbm = pl.BlockSpec(memory_space=pltpu.HBM)
    return pl.pallas_call(
        project_kernel,
        out_shape=jax.ShapeDtypeStruct((ROWS, half_w), BF),
        in_specs=[SMEM, VMEM, VMEM, hbm, hbm, VMEM],
        out_specs=hbm,
        scratch_shapes=[
            pltpu.VMEM((steps, 1024, cols), BF),
            pltpu.VMEM((steps, 1024, cols), BF),
            pltpu.VMEM((steps, ROWS, cols), BF),
            pltpu.SemaphoreType.DMA((3, steps)),
        ],
        compiler_params=params(32),
        name="project",
    )(hd.reshape(1), o_home, o_other, weight, w_other, gain)


def solution(mesh):
    return jax.shard_map(
        local,
        mesh=mesh,
        in_specs=(
            P("ctx", "head"),
            P("ctx", "head"),
            P("ctx", "head"),
            P("head", None),
            P("ctx"),
            P("ctx"),
            P("ctx"),
        ),
        out_specs=P("ctx", "head"),
        check_vma=False,
    )
```

```python
import functools

import jax
import jax.numpy as jnp
import numpy as np
from jax import lax
from jax.experimental import pallas as pl
from jax.experimental.pallas import tpu as pltpu
from jax.sharding import PartitionSpec as P

HEAD_WIDTH = 128
THETA = 500000.0
CAP = 320
SLOTS = 8
SHARDS = 128
ROWS = 512
T = 64
N = CAP // T
TILES = N + 1
REACH = (80, 144, 208, 272, 272, 272)
MORE = 16
BIG = float(1 << 30)
LOW = -1e30
EXTRA = 16
BF = jnp.bfloat16
F32 = jnp.float32
SCALE2 = float(1.0 / np.sqrt(128.0) * np.log2(np.e))
VMEM = pl.BlockSpec(memory_space=pltpu.VMEM)
SMEM = pl.BlockSpec(memory_space=pltpu.SMEM)


def params(mib):
    return pltpu.CompilerParams(vmem_limit_bytes=mib * 2**20)


def perm_of(axis, k):
    pairs = []
    for d in range(SHARDS):
        z, x, y = d // 16, d // 4 % 4, d % 4
        if axis == "z":
            z = (z + k) % 8
        elif axis == "x":
            x = (x + k) % 4
        else:
            y = y ^ 1
        pairs.append((d, z * 16 + x * 4 + y))
    return pairs


def hop(a, axis, k=1):
    return lax.ppermute(a, "ctx", perm_of(axis, k))


def ring(a, axis, size, row_dim):
    half = a.shape[row_dim] // 2
    out, up, down = [a], a, a
    for _ in range(size // 2 - 1):
        up, down = hop(up, axis, 1), hop(down, axis, -1)
        out += [up, down]
    lo = hop(lax.slice_in_dim(up, 0, half, axis=row_dim), axis, 1)
    hi = hop(lax.slice_in_dim(down, half, 2 * half, axis=row_dim), axis, -1)
    out.append(jnp.concatenate([lo, hi], axis=row_dim))
    return out


def ring_steps(size):
    steps = [0]
    for i in range(1, size // 2):
        steps += [-i, i]
    return steps + [size // 2]


def pack_matrix(rot, transpose):
    packed_dim = 1 if transpose else 0
    o = lax.broadcasted_iota(jnp.int32, (ROWS, ROWS), packed_dim)
    s = lax.broadcasted_iota(jnp.int32, (ROWS, ROWS), 1 - packed_dim)
    src = (o & 7) * 64 + (((o >> 3) + 64 - rot) & 63)
    return jnp.where(src == s, 1.0, 0.0).astype(BF)


def pack_kernel(rot_ref, q_ref, k_ref, v_ref, cos_ref, sin_ref, out_ref):
    cos, sin = cos_ref[...], sin_ref[...]

    def rotate(x):
        x = x.astype(F32)
        return (x * cos + pltpu.roll(x, 64, 1) * sin).astype(BF)

    m = pack_matrix(rot_ref[0], False)
    parts = [rotate(q_ref[:, g * 128 : (g + 1) * 128]) for g in range(4)]
    parts += [rotate(k_ref[...]), v_ref[...]]
    for c, x in enumerate(parts):
        y = jnp.dot(m, x, preferred_element_type=F32).astype(BF)
        out_ref[:, 0, :, c * 128 : (c + 1) * 128] = y.reshape(32, 16, 128)


def compact_matrix(pos):
    p = lax.broadcasted_iota(jnp.int32, (CAP, SHARDS * SLOTS), 0)
    return jnp.where(p == pos, 1.0, 0.0).astype(BF)


def columns(i):
    if i < N - 1:
        return [(i * T, T, g) for g in range(4)]
    return [(i * T + b * 32, 32, g) for b in range(2) for g in range(4)]


def compact_kernel(pos_ref, x_ref, kv_ref, q_ref):
    m = compact_matrix(pos_ref[...])
    kv_ref[...] = jnp.dot(m, x_ref[:, 512:], preferred_element_type=F32).astype(BF)
    y = jnp.dot(m, x_ref[:, :512], preferred_element_type=F32).astype(BF)
    for i in range(N):
        at = 0
        for row, rows, g in columns(i):
            q_ref[i, at : at + rows, :] = y[row : row + rows, g * 128 : (g + 1) * 128]
            at += rows


def attend_kernel(n, first, last, *refs):
    more_ref, live_ref, qid_ref, kid_ref, qa_ref, qb_ref = refs[:6]
    kv_refs, refs = refs[6 : 6 + n], refs[6 + n :]
    if not first:
        refs = refs[2:]
    ml_ref, acc_ref = refs[:2]
    if first:
        row = lax.broadcasted_iota(jnp.int32, ml_ref.shape, 2)
        ml_ref[...] = jnp.where(row == 0, LOW, 0.0)
        acc_ref[...] = jnp.zeros_like(acc_ref)

    def batch(tiles, start, rows):
        at = pl.ds(start, rows)
        keys = [kv[:, at, :128].reshape(4 * rows, 128) for kv in kv_refs]
        vals = [kv[:, at, 128:].reshape(4 * rows, 128) for kv in kv_refs]
        kids = []
        for c in range(n):
            col = kid_ref[c, :, at, :].reshape(4 * rows, 128)
            kids.append(jnp.concatenate([col, col], axis=1))
        old = [(ml_ref[h, i, 0:1, :], ml_ref[h, i, 1:2, :], acc_ref[h, i]) for _, _, h, i in tiles]
        found = []
        for (q, qid, _, _), (m, _, _) in zip(tiles, old):
            scores = []
            for key, kid in zip(keys, kids):
                s = lax.dot_general(key, q, (((1,), (1,)), ((), ())), preferred_element_type=F32)
                s = jnp.where(kid <= qid, s, LOW)
                m = jnp.maximum(m, jnp.max(s, axis=0, keepdims=True))
                scores.append(s)
            found.append((scores, m))
        done = []
        for (scores, new), (m, total, acc) in zip(found, old):
            keep = jnp.exp2((m - new) * SCALE2)
            total, acc = total * keep, acc * keep
            for s, val in zip(scores, vals):
                p = jnp.exp2((s - new) * SCALE2)
                total = total + jnp.sum(p, axis=0, keepdims=True)
                acc = acc + lax.dot_general(
                    val, p.astype(BF), (((0,), (0,)), ((), ())), preferred_element_type=F32
                )
            done.append((new, total, acc))
        for (_, _, h, i), (m, total, acc) in zip(tiles, done):
            ml_ref[h, i, 0:1, :] = m
            ml_ref[h, i, 1:2, :] = total
            acc_ref[h, i] = acc

    def visit(i):
        if i < N - 1:
            tiles = [(qa_ref[i], qid_ref[0, i], 0, i), (qb_ref[i], qid_ref[1, i], 1, i)]
        else:
            b = i - (N - 1)
            c = slice(b * 128, (b + 1) * 128)
            q = jnp.concatenate([qa_ref[N - 1, c], qb_ref[N - 1, c]], axis=0)
            qid = jnp.concatenate([qid_ref[0, N - 1, :, c], qid_ref[1, N - 1, :, c]], axis=1)
            tiles = [(q, qid, b, N - 1)]
        batch(tiles, 0, REACH[i])

        def further(e, _):
            batch(tiles, pl.multiple_of(REACH[i] + e * MORE, MORE), MORE)
            return 0

        lax.fori_loop(0, more_ref[i], further, 0)

    for i in range(TILES):
        if i < N - 1:
            visit(i)
        else:
            pl.when(live_ref[i] > 0)(functools.partial(visit, i))
    if last:
        for i in range(N):
            o, lse = of_half(1, i, ml_ref, acc_ref)
            hi = lse.astype(BF).astype(F32)
            mid = (lse - hi).astype(BF).astype(F32)
            lo = lse - hi - mid
            row = lax.broadcasted_iota(jnp.int32, (EXTRA, 4 * T), 0)
            note = jnp.where(row == 0, hi, jnp.where(row == 1, mid, jnp.where(row == 2, lo, 0.0)))
            refs[2][i, :128, :] = o.astype(BF)
            refs[2][i, 128:, :] = note.astype(BF)


def of_half(half, i, ml_ref, acc_ref):
    if i < N - 1:
        return finish(ml_ref[half, i], acc_ref[half, i])
    c = slice(half * 128, (half + 1) * 128)
    ml = jnp.concatenate([ml_ref[0, i, :, c], ml_ref[1, i, :, c]], axis=1)
    acc = jnp.concatenate([acc_ref[0, i, :, c], acc_ref[1, i, :, c]], axis=1)
    return finish(ml, acc)


def finish(ml, acc):
    m, total = ml[0:1], ml[1:2]
    some = total > 0.0
    total = jnp.where(some, total, 1.0)
    lse = jnp.where(some, m * SCALE2 + jnp.log2(total), LOW)
    return acc / total, lse


def merge_kernel(post_ref, ml_ref, acc_ref, got_ref, out_ref, ob_ref):
    for i in range(N):
        mine, lse_a = of_half(0, i, ml_ref, acc_ref)
        got = got_ref[i].astype(F32)
        lse_b = got[128:129] + got[129:130] + got[130:131]
        top = jnp.maximum(lse_a, lse_b)
        wa, wb = jnp.exp2(lse_a - top), jnp.exp2(lse_b - top)
        inv = 1.0 / (wa + wb)
        o = (mine * (wa * inv) + got[:128] * (wb * inv)).T.astype(BF)
        at = 0
        for row, rows, g in columns(i):
            ob_ref[row : row + rows, g * 128 : (g + 1) * 128] = o[at : at + rows]
            at += rows
    p = lax.broadcasted_iota(jnp.int32, (SHARDS * SLOTS, CAP), 1)
    spread = jnp.where(p == post_ref[...], 1.0, 0.0).astype(BF)
    out_ref[...] = jnp.dot(spread, ob_ref[...], preferred_element_type=F32).astype(BF)


def home_kernel(rot_ref, o_ref, out_ref):
    m = pack_matrix(rot_ref[0], True)
    for h in range(2):
        x = o_ref[:, h, :, :].reshape(ROWS, 512)
        out_ref[:, h * 512 : (h + 1) * 512] = jnp.dot(m, x, preferred_element_type=F32).astype(BF)


def project_kernel(
    hd_ref, own_ref, other_ref, wa_ref, wb_ref, gain_ref, out_ref, a_ref, b_ref, o_ref, sems
):
    n, cols = o_ref.shape[0], o_ref.shape[2]
    first = pl.multiple_of(hd_ref[0] * (n * cols), n * cols)
    loads = []
    for i in range(n):
        mine = wa_ref.at[:, pl.ds(first + i * cols, cols)]
        a = pltpu.make_async_copy(mine, a_ref.at[i], sems.at[0, i])
        theirs = wb_ref.at[:, pl.ds(i * cols, cols)]
        b = pltpu.make_async_copy(theirs, b_ref.at[i], sems.at[1, i])
        a.start()
        b.start()
        loads.append((a, b))
    gain = gain_ref[:, :1]
    stores = []
    for i, (a, b) in enumerate(loads):
        a.wait()
        s = jnp.dot(own_ref[...], a_ref[i], preferred_element_type=F32)
        b.wait()
        s = s + jnp.dot(other_ref[...], b_ref[i], preferred_element_type=F32)
        s = s.astype(BF).astype(F32)
        o_ref[i] = jnp.where(gain != 0.0, gain * s, 0.0).astype(BF)
        out = out_ref.at[:, pl.ds(i * cols, cols)]
        store = pltpu.make_async_copy(o_ref.at[i], out, sems.at[2, i])
        store.start()
        stores.append(store)
    for store in stores:
        store.wait()


def local(q_home, k_home, v_home, weight, router, positions, counts):
    d = lax.axis_index("ctx").astype(jnp.int32)
    hd = lax.axis_index("head").astype(jnp.int32)
    half_w = weight.shape[1] // 2

    to_send = lax.dynamic_slice_in_dim(weight, (1 - hd) * half_w, half_w, axis=1)
    own_live = jnp.arange(ROWS, dtype=jnp.int32) < counts[0]
    gain = jnp.broadcast_to(jnp.where(own_live, router, 0.0)[:, None], (ROWS, 128))
    to_send, gain = lax.optimization_barrier((to_send, gain))
    w_other = lax.ppermute(to_send, "head", [(0, 1), (1, 0)])

    freqs = THETA ** (-(jnp.arange(64, dtype=F32) * 2.0 / HEAD_WIDTH))
    angles = positions.astype(F32)[:, None] * jnp.concatenate([freqs, freqs])[None, :]
    sign = jnp.where(jnp.arange(128) < 64, -1.0, 1.0).astype(F32)
    cos, sin = jnp.cos(angles), jnp.sin(angles) * sign[None, :]
    rot = (d % 64).reshape(1)

    packed = pl.pallas_call(
        pack_kernel,
        out_shape=jax.ShapeDtypeStruct((32, 2, 16, 768), BF),
        grid=(2,),
        in_specs=[
            SMEM,
            pl.BlockSpec((ROWS, 512), lambda h: (0, h)),
            pl.BlockSpec((ROWS, 128), lambda h: (0, h)),
            pl.BlockSpec((ROWS, 128), lambda h: (0, h)),
            pl.BlockSpec((ROWS, 128), lambda h: (0, 0)),
            pl.BlockSpec((ROWS, 128), lambda h: (0, 0)),
        ],
        out_specs=pl.BlockSpec((32, 1, 16, 768), lambda h: (0, h, 0, 0)),
        compiler_params=params(56),
        name="pack",
    )(rot, q_home, k_home, v_home, cos, sin)
    got = lax.all_to_all(packed.reshape(1024, 768), "ctx", 0, 0, tiled=True)
    all_counts = lax.all_gather(counts, "ctx", axis=0, tiled=True)

    z, x, yl = d // 16, d // 4 % 4, d % 2
    dz = jnp.asarray(np.array(ring_steps(8), np.int32))
    dx = jnp.asarray(np.array(ring_steps(4), np.int32))
    member = ((z + dz) % 8)[:, None] * 8 + ((x + dx) % 4)[None, :] * 2 + yl
    partner = z * 8 + x * 2 + (1 - yl)
    member = jnp.concatenate([member.reshape(32), partner.reshape(1)])
    shard = jnp.arange(SHARDS, dtype=jnp.int32)

    def layout(who, all_counts):
        offset = (who[:, None] - shard[None, :]) % 64
        held = jnp.maximum((all_counts[None, :] - offset + 63) // 64, 0)
        before = (shard[:, None] < shard[None, :]).astype(BF)
        start = jnp.dot(held.astype(BF), before, preferred_element_type=F32).astype(jnp.int32)
        return offset, held, start

    _, held, start = layout(member[:1], all_counts)
    slot = jnp.arange(SLOTS, dtype=jnp.int32)[None, :]
    pos = jnp.where(slot < held[0][:, None], start[0][:, None] + slot, -1).reshape(-1)
    kv_own, q_own = pl.pallas_call(
        compact_kernel,
        out_shape=(
            jax.ShapeDtypeStruct((CAP, 256), BF),
            jax.ShapeDtypeStruct((N, 4 * T, 128), BF),
        ),
        in_specs=[VMEM] * 2,
        out_specs=(VMEM, VMEM),
        compiler_params=params(16),
        name="compact",
    )(pos[None, :], got)
    kv_own, q_own, counts_now = lax.optimization_barrier((kv_own, q_own, all_counts))
    q_partner = hop(q_own, "y")
    slab = jnp.stack(ring(kv_own, "x", 4, 0))
    slab, q_partner = lax.optimization_barrier((slab, q_partner))
    slabs = ring(slab, "z", 8, 1)

    offset, held, start = layout(member, counts_now)
    base = (shard[None, :] * ROWS + offset - 64 * start).astype(F32)
    place = jnp.arange(CAP, dtype=jnp.int32)[None, None, :]
    inside = (start[:, :, None] <= place) & (place < (start + held)[:, :, None])
    ids = jnp.sum(jnp.where(inside, base[:, :, None] + (64 * place).astype(F32), 0.0), axis=1)
    ids = jnp.where(place[0] < jnp.sum(held, axis=1)[:, None], ids, BIG)
    q_rows = jnp.stack([ids[0], ids[32]])
    best = jnp.max(jnp.where(q_rows >= BIG, -1.0, q_rows), axis=0)
    tile_of = np.minimum(np.arange(CAP) // T, N - 1) + (np.arange(CAP) >= CAP - 32)
    here = jnp.asarray(tile_of[None, :] == np.arange(TILES)[:, None])
    q_max = jnp.max(jnp.where(here, best[None, :], -1.0), axis=1)
    live = (q_max >= 0.0).astype(jnp.int32)
    reach = jnp.sum((ids[:32, None, :] <= q_max[None, :, None]).astype(jnp.int32), axis=2)
    reach = jnp.max(reach.reshape(8, 4, TILES), axis=1)
    more = jnp.maximum(reach - jnp.asarray(REACH, jnp.int32)[None, :] + MORE - 1, 0) // MORE
    q_tiles = q_rows[:, : CAP - T].reshape(2, N - 1, 1, T)
    q_ids = jnp.tile(q_tiles[:, :, :, :], (1, 1, 4, 1)).reshape(2, N - 1, 1, 4 * T)
    q_last = jnp.tile(q_rows[:, CAP - T :].reshape(2, 2, 1, 32), (1, 1, 4, 1))
    q_ids = jnp.concatenate([q_ids, q_last.reshape(2, 1, 1, 4 * T)], axis=1)
    slab_ids = ids[:32].reshape(8, 4, CAP, 1)

    state = ()
    chunks = ((0,), (1, 2), (3, 4), (5, 6), (7,))
    for c, chunk in enumerate(chunks):
        first, last, n = c == 0, c == len(chunks) - 1, len(chunk)
        steps = jnp.max(more[chunk[0] : chunk[-1] + 1], axis=0)
        k_ids = jnp.broadcast_to(slab_ids[chunk[0] : chunk[-1] + 1], (n, 4, CAP, 128))
        shapes = [
            jax.ShapeDtypeStruct((2, N, 8, 4 * T), F32),
            jax.ShapeDtypeStruct((2, N, 128, 4 * T), F32),
        ]
        if last:
            shapes.append(jax.ShapeDtypeStruct((N, 128 + EXTRA, 4 * T), BF))
        state = pl.pallas_call(
            functools.partial(attend_kernel, n, first, last),
            out_shape=tuple(shapes),
            in_specs=[SMEM] * 2 + [VMEM] * (4 + n + len(state)),
            out_specs=(VMEM,) * len(shapes),
            input_output_aliases={} if first else {6 + n: 0, 7 + n: 1},
            compiler_params=params(48),
            cost_estimate=pl.CostEstimate(
                flops=n * 4_000_000_000, bytes_accessed=n * 4_000_000, transcendentals=n * 2_000_000
            ),
            name="attend",
        )(steps, live, q_ids, k_ids, q_own, q_partner, *[slabs[k] for k in chunk], *state)
    ml, acc, message = state
    theirs = hop(message, "y")

    o_packed = pl.pallas_call(
        merge_kernel,
        out_shape=jax.ShapeDtypeStruct((1024, 512), BF),
        in_specs=[VMEM] * 4,
        out_specs=VMEM,
        scratch_shapes=[pltpu.VMEM((CAP, 512), BF)],
        compiler_params=params(24),
        name="merge",
    )(pos[:, None], ml, acc, theirs)

    o_got = lax.all_to_all(o_packed, "ctx", 0, 0, tiled=True)
    o_home = pl.pallas_call(
        home_kernel,
        out_shape=jax.ShapeDtypeStruct((ROWS, 1024), BF),
        in_specs=[SMEM, VMEM],
        out_specs=VMEM,
        compiler_params=params(16),
        name="home",
    )(rot, o_got.reshape(32, 2, 16, 512))
    o_other = lax.ppermute(o_home, "head", [(0, 1), (1, 0)])

    cols = 512
    steps = half_w // cols
    hbm = pl.BlockSpec(memory_space=pltpu.HBM)
    return pl.pallas_call(
        project_kernel,
        out_shape=jax.ShapeDtypeStruct((ROWS, half_w), BF),
        in_specs=[SMEM, VMEM, VMEM, hbm, hbm, VMEM],
        out_specs=hbm,
        scratch_shapes=[
            pltpu.VMEM((steps, 1024, cols), BF),
            pltpu.VMEM((steps, 1024, cols), BF),
            pltpu.VMEM((steps, ROWS, cols), BF),
            pltpu.SemaphoreType.DMA((3, steps)),
        ],
        compiler_params=params(52),
        name="project",
    )(hd.reshape(1), o_home, o_other, weight, w_other, gain)


def solution(mesh):
    return jax.shard_map(
        local,
        mesh=mesh,
        in_specs=(
            P("ctx", "head"),
            P("ctx", "head"),
            P("ctx", "head"),
            P("head", None),
            P("ctx"),
            P("ctx"),
            P("ctx"),
        ),
        out_specs=P("ctx", "head"),
        check_vma=False,
    )
```
